256 devices in a mesh: row: 16 (over x, z_lo, core), col: 16 (over z_hi, y).
Axes of the slice: x: 4, y: 4, z: 8 (z_hi: 4, z_lo: 2; z = z_hi * 2 + z_lo), core: 2. Of those that a mesh axis runs over, the one named last changes fastest.
Arguments:
- frames_in: bfloat16 [4, 128, 128, 256], P(None, 'row', 'col'), may hold values from -6 to 6
- norm_gain: float32 [256], replicated, may hold values from 0.1 to 1.9
- first_kernel: bfloat16 [3, 3, 3, 256, 256], replicated, may hold values from -0.078125 to 0.078125
- second_kernel: bfloat16 [3, 3, 3, 256, 256], replicated, may hold values from -0.078125 to 0.078125
- latent_kernel: bfloat16 [3, 3, 4096, 1024], P(None, None, None, 'col'), may hold values from -0.03125 to 0.03125
Outputs:
- encoded: bfloat16 [4, 32, 32, 1024], P(None, 'row', None, 'col')
The draws below stay inside these ranges and needn't reach their ends.
All inputs are finite; a program needn't handle non-finite values.
Results may differ from the reference program's by a relative error of at most 0.0053.
Values may be sent and summed in bfloat16 or wider, within the bound.
A program may use at most 128 MiB of HBM per device.

```python
import jax
import jax.numpy as jnp
from jax import lax

FRAMES = 4
WIDTH = 256
OUT_CH = 1024
LATENT = 4096
HEIGHT = 128
BREADTH = 128


def shard_levels(key, extent, shards, least, largest):
    def one(position, parts):
        steps = jax.random.uniform(jax.random.fold_in(jax.random.fold_in(key, 6), position), (parts,), jnp.float32, least / len(shards), largest / len(shards))
        return jnp.repeat(jnp.exp(steps), extent[position] // parts).reshape((-1,) + (1,) * (len(extent) - position - 1))

    level = one(*shards[0])
    for cut in shards[1:]:
        level = level * one(*cut)
    return level


def gaussian(key, dims, deviation, most, shards=(), kind=jnp.bfloat16):
    gain = shard_levels(key, dims, shards, -0.22, 0.18) if shards else 1.0
    drawn = jax.random.normal(key, dims, jnp.float32) * deviation * gain
    return jnp.minimum(jnp.maximum(drawn, -most), most).astype(kind)


def setup_inputs(seed: int = 0) -> dict:
    arg_keys = jax.random.split(jax.random.key(seed), 6)
    frames_in = gaussian(arg_keys[0], (FRAMES, HEIGHT, BREADTH, WIDTH), 1.0, 6.0, ((1, 16), (2, 16)))
    norm_gain = jnp.clip(1.0 + 0.18 * jax.random.normal(arg_keys[1], (WIDTH,), jnp.float32), 0.1, 1.9)
    first_kernel = gaussian(arg_keys[2], (3, 3, 3, WIDTH, WIDTH), (27 * WIDTH) ** -0.5, 0.078125)
    second_kernel = gaussian(arg_keys[3], (3, 3, 3, WIDTH, WIDTH), (27 * WIDTH) ** -0.5, 0.078125)
    latent_kernel = gaussian(arg_keys[4], (3, 3, LATENT, OUT_CH), (9 * LATENT) ** -0.5, 0.03125, ((3, 16),))
    return dict(frames_in=frames_in, norm_gain=norm_gain, first_kernel=first_kernel, second_kernel=second_kernel, latent_kernel=latent_kernel)


def conv_volume(field, kernel):
    frames, rows, cols, chans = field.shape
    padded = jnp.pad(field, ((1, 1), (1, 1), (1, 1), (0, 0)))
    total = jnp.zeros((frames * rows * cols, kernel.shape[4]), jnp.float32)
    for a in range(3):
        for b in range(3):
            for e in range(3):
                piece = padded[a:a + frames, b:b + rows, e:e + cols].reshape(-1, chans)
                total = total + jnp.dot(piece, kernel[a, b, e], preferred_element_type=jnp.float32)
    return total.reshape(frames, rows, cols, -1)

def reference(frames_in, norm_gain, first_kernel, second_kernel, latent_kernel):
    values = frames_in.astype(jnp.float32)
    scale = lax.rsqrt(lax.optimization_barrier(jnp.mean(values * values, axis=-1, keepdims=True)) + 1e-06)
    normed = (values * scale * norm_gain).astype(jnp.bfloat16)
    hidden = jax.nn.silu(conv_volume(normed, first_kernel)).astype(jnp.bfloat16)
    mixed = (values + conv_volume(hidden, second_kernel)).astype(jnp.bfloat16)
    frames, rows, cols, chans = mixed.shape
    latent = mixed.reshape(frames, rows // 4, 4, cols // 4, 4, chans)
    latent = latent.transpose(0, 1, 3, 2, 4, 5).reshape(frames, rows // 4, cols // 4, 16 * chans)
    lrows, lcols = (rows // 4, cols // 4)
    padded = jnp.pad(latent, ((0, 0), (1, 1), (1, 1), (0, 0)))
    total = jnp.zeros((frames * lrows * lcols, OUT_CH), jnp.float32)
    for b in range(3):
        for e in range(3):
            piece = padded[:, b:b + lrows, e:e + lcols].reshape(-1, LATENT)
            total = total + jnp.dot(piece, latent_kernel[b, e], preferred_element_type=jnp.float32)
    group = LATENT // OUT_CH
    shortcut = lax.optimization_barrier(jnp.mean(latent.astype(jnp.float32).reshape(frames, lrows, lcols, OUT_CH, group), axis=-1))
    encoded = total.reshape(frames, lrows, lcols, OUT_CH) + shortcut
    return encoded.astype(jnp.bfloat16)
```

```python
import functools

import jax
import jax.numpy as jnp
import numpy as np
from jax import lax
from jax.experimental import pallas as pl
from jax.experimental.pallas import tpu as pltpu
from jax.sharding import PartitionSpec as P

MESH = pl.DeviceIdType.MESH
F32 = jnp.float32
BF16 = jnp.bfloat16
FRAMES, SIDE, CHANS = 4, 8, 256
OUT_CH, LATENT = 1024, 4096
RING = 4
PIECES = RING * RING
CHUNKS = 8
CHUNK = LATENT // CHUNKS
OUT_DEV = OUT_CH // PIECES
Y_FIRST = (False,) * CHUNKS


def one_hot(index, width):
    out = np.zeros((len(index), width), np.float32)
    for at, source in enumerate(index):
        if source >= 0:
            out[at, source] = 1
    return out.astype(BF16)


def spread_tables():
    own, halo = [], []
    for p in range(-2, 6):
        for q in range(-2, 6):
            for i in range(2):
                for f in range(FRAMES):
                    for j in range(2):
                        r, c = 4 * i + p, 4 * j + q
                        inside_r, inside_c = 0 <= r < SIDE, 0 <= c < SIDE
                        a, b = -1, -1
                        side = 0 if c < 0 else 1
                        cc = c + 2 if c < 0 else c - SIDE
                        rr = r + 2 if r < 0 else r - SIDE
                        if inside_r and inside_c:
                            a = f * 64 + r * 8 + c
                        elif inside_c:
                            b = ((0 if r < 0 else 4) + f) * 16 + rr * 8 + c
                        elif inside_r:
                            b = (8 + 4 * side + r // 2) * 16 + f * 4 + (r % 2) * 2 + cc
                        else:
                            b = (16 + (0 if r < 0 else 2) + side) * 16 + f * 4 + rr * 2 + cc
                        own.append(a)
                        halo.append(b)
    return one_hot(own, 256), one_hot(halo, 384)


def strip_table():
    index = []
    for side in range(2):
        for rp in range(4):
            for f in range(FRAMES):
                for rr in range(2):
                    for cc in range(2):
                        index.append(f * 64 + (2 * rp + rr) * 8 + 6 * side + cc)
    return one_hot(index, 256)


def mean_table():
    group = LATENT // OUT_CH
    out = np.zeros((CHANS, CHANS // group), np.float32)
    out[np.arange(CHANS), np.arange(CHANS) // group] = 1 / group
    return out.astype(BF16)


def convolve(src, w, n, acc):
    rows = n * n * 16
    for a in range(3):
        total = None
        for b in range(3):
            for e in range(3):
                part = jnp.dot(src[b : b + n, e : e + n].reshape(rows, CHANS), w[a, b, e], preferred_element_type=F32)
                total = part if total is None else total + part
        acc[a, :rows] = total


def joined(acc, rows):
    early, same, late = (acc[a, :rows].reshape(rows // 8, 8, CHANS) for a in range(3))
    f = lax.broadcasted_iota(jnp.int32, (1, 8, CHANS), 1) // 2
    return same + jnp.where(f > 0, pltpu.roll(early, 2, 1), 0.0) + jnp.where(f < FRAMES - 1, pltpu.roll(late, 6, 1), 0.0)


def kernel(
    n_row, n_col,
    x_hbm, gain_hbm, k1_hbm, k2_hbm, w_hbm, g_own_hbm, g_halo_hbm, g_strip_hbm, g_mean_hbm,
    out_ref,
    x, gain, k1, k2, w, g_own, g_halo, g_strip, g_mean,
    strips, halo, normed, cells, hidden, acc, lat, y_acc, u_out, u_in, kept,
    load_sem, w_sem, halo_send, halo_recv,
    near_send, near_recv, far_send, far_recv, near2_send, near2_recv, far2_send, far2_recv,
    u_send, u_recv,
):
    row, col = lax.axis_index("row"), lax.axis_index("col")
    zh, y = col // RING, col % RING
    up, down = lax.rem(row + n_row - 1, n_row), lax.rem(row + 1, n_row)
    left, right = lax.rem(col + n_col - 1, n_col), lax.rem(col + 1, n_col)
    z_next, z_prev = lax.rem(zh + 1, RING), lax.rem(zh + RING - 1, RING)
    y_next, y_prev = lax.rem(y + 1, RING), lax.rem(y + RING - 1, RING)
    to_z = ((row, z_next * RING + y), (row, z_prev * RING + y))
    to_y = ((row, zh * RING + y_next), (row, zh * RING + y_prev))

    barrier = pltpu.get_barrier_semaphore()
    around = (
        (up, col), (down, col), (row, left), (row, right),
        (up, left), (up, right), (down, left), (down, right),
    ) + to_z + to_y
    for target in around:
        pl.semaphore_signal(barrier, inc=1, device_id=target, device_id_type=MESH)

    loads = []
    for at, (source, target) in enumerate((
        (x_hbm, x), (g_strip_hbm, g_strip), (gain_hbm, gain), (g_own_hbm, g_own), (g_halo_hbm, g_halo),
        (k1_hbm, k1), (k2_hbm, k2), (g_mean_hbm, g_mean),
    )):
        copy = pltpu.make_async_copy(source, target, load_sem.at[at])
        copy.start()
        loads.append(copy)
    w_loads = []
    for b in range(3):
        for e in range(3):
            copy = pltpu.make_async_copy(w_hbm.at[b, e], w.at[e, pl.ds(b * OUT_DEV, OUT_DEV)], w_sem.at[b * 3 + e])
            copy.start()
            w_loads.append(copy)
    load_x, load_strip, load_gain, load_own, load_halo, load_k1, load_k2, load_mean = loads

    def send(source, target, send_sem, recv_sem, device):
        copy = pltpu.make_async_remote_copy(
            src_ref=source, dst_ref=target, send_sem=send_sem, recv_sem=recv_sem, device_id=device, device_id_type=MESH
        )
        copy.start()
        return copy

    load_x.wait()
    pl.semaphore_wait(barrier, len(around))
    sent = [
        send(x.at[:, 0], halo.at[pl.ds(4, 4)], halo_send.at[0], halo_recv.at[0], (up, col)),
        send(x.at[:, 3], halo.at[pl.ds(0, 4)], halo_send.at[1], halo_recv.at[1], (down, col)),
    ]
    load_strip.wait()
    own = x[...].reshape(256, CHANS)
    strips[...] = jnp.dot(g_strip[...], own, preferred_element_type=F32).astype(BF16).reshape(2, 4, 16, CHANS)
    sent += [
        send(strips.at[0, 3], halo.at[17], halo_send.at[4], halo_recv.at[4], (down, left)),
        send(strips.at[1, 3], halo.at[16], halo_send.at[5], halo_recv.at[5], (down, right)),
        send(strips.at[0, 0], halo.at[19], halo_send.at[6], halo_recv.at[6], (up, left)),
        send(strips.at[1, 0], halo.at[18], halo_send.at[7], halo_recv.at[7], (up, right)),
        send(strips.at[0], halo.at[pl.ds(12, 4)], halo_send.at[2], halo_recv.at[2], (row, left)),
        send(strips.at[1], halo.at[pl.ds(8, 4)], halo_send.at[3], halo_recv.at[3], (row, right)),
    ]

    load_gain.wait()

    def norm(raw):
        values = raw.astype(F32)
        scale = lax.rsqrt(jnp.mean(values * values, axis=-1, keepdims=True) + 1e-06)
        return values * scale * gain[...]

    normed[0:16] = norm(own).astype(BF16).reshape(16, 16, CHANS)
    normed[36:40] = jnp.zeros((4, 16, CHANS), BF16)
    load_own.wait()
    middle = g_own[...].reshape(8, 8, 16, 256)[2:6, 2:6].reshape(256, 256)
    kept[...] = jnp.dot(middle, own, preferred_element_type=F32)

    for copy in sent:
        copy.wait_recv()
    has_up, has_down = row > 0, row < n_row - 1
    has_left, has_right = col > 0, col < n_col - 1
    for start, count, there in (
        (0, 4, has_up), (4, 4, has_down), (8, 4, has_left), (12, 4, has_right),
        (16, 1, has_up & has_left), (17, 1, has_up & has_right),
        (18, 1, has_down & has_left), (19, 1, has_down & has_right),
    ):
        values = norm(halo[start : start + count].reshape(count * 16, CHANS))
        values = values * jnp.where(there, 1.0, 0.0).astype(F32)
        normed[16 + start : 16 + start + count] = values.astype(BF16).reshape(count, 16, CHANS)
    load_halo.wait()
    spread = jnp.dot(g_own[...], normed[0:16].reshape(256, CHANS), preferred_element_type=F32)
    spread += jnp.dot(g_halo[...], normed[16:40].reshape(384, CHANS), preferred_element_type=F32)
    cells[...] = spread.astype(BF16).reshape(8, 8, 16, CHANS)

    load_k1.wait()
    convolve(cells, k1, 6, acc)
    value = joined(acc, 576)
    value = (value / (1.0 + jnp.exp(-value))).reshape(6, 6, 2, 8, CHANS)
    hidden[...] = value.astype(BF16).reshape(6, 6, 16, CHANS)
    place = lax.broadcasted_iota(jnp.int32, (1, 16, CHANS), 1)
    i_of, j_of = place // 8, place % 2
    none = jnp.zeros((), BF16)
    for edge, outside, there in ((0, i_of == 0, has_up), (5, i_of == 1, has_down)):
        keep = jnp.logical_or(jnp.logical_not(outside), there)
        hidden[edge] = jnp.where(keep, hidden[edge].astype(F32), 0.0).astype(BF16)
    for edge, outside, there in ((0, j_of == 0, has_left), (5, j_of == 1, has_right)):
        keep = jnp.logical_or(jnp.logical_not(outside), there)
        hidden[:, edge] = jnp.where(keep, hidden[:, edge].astype(F32), 0.0).astype(BF16)

    load_k2.wait()
    convolve(hidden, k2, 4, acc)
    mixed = (kept[...].reshape(32, 8, CHANS) + joined(acc, 256)).astype(BF16).reshape(16, 16, CHANS)
    for tile in range(16):
        lat[tile // 2, zh, y, :, (tile % 2) * CHANS : (tile % 2 + 1) * CHANS] = mixed[tile]

    opposite_z, opposite_y = lax.rem(zh + 2, RING), lax.rem(y + 2, RING)
    pending = []
    near, far, near2, far2 = [None] * CHUNKS, [None] * CHUNKS, [None] * CHUNKS, [None] * CHUNKS
    for h in range(CHUNKS):
        piece = lat.at[h, zh, y]
        targets = to_y if Y_FIRST[h] else to_z
        near[h] = [
            send(piece, piece, near_send.at[h, d], near_recv.at[h, d], targets[d]) for d in range(2)
        ]
        pending += near[h]

    def relay_piece(h):
        forward = h % 2 == 0
        if Y_FIRST[h]:
            return lat.at[h, zh, y_prev if forward else y_next], to_y[0 if forward else 1]
        return lat.at[h, z_prev if forward else z_next, y], to_z[0 if forward else 1]

    def group(h, which):
        if Y_FIRST[h]:
            return lat.at[h, (z_prev, zh, z_next)[which + 1]]
        return lat.at[h, :, (y_prev, y, y_next)[which + 1]]

    for step in range(CHUNKS + 3):
        h = step
        if h < CHUNKS:
            for copy in near[h]:
                copy.wait_recv()
            piece, device = relay_piece(h)
            far[h] = send(piece, piece, far_send.at[h], far_recv.at[h], device)
            pending.append(far[h])
        h = step - 1
        if 0 <= h < CHUNKS:
            far[h].wait_recv()
            targets = to_z if Y_FIRST[h] else to_y
            piece = group(h, 0)
            near2[h] = [
                send(piece, piece, near2_send.at[h, d], near2_recv.at[h, d], targets[d]) for d in range(2)
            ]
            pending += near2[h]
        h = step - 2
        if 0 <= h < CHUNKS:
            for copy in near2[h]:
                copy.wait_recv()
            targets = to_z if Y_FIRST[h] else to_y
            forward = h % 2 == 0
            piece = group(h, -1 if forward else 1)
            far2[h] = send(piece, piece, far2_send.at[h], far2_recv.at[h], targets[0 if forward else 1])
            pending.append(far2[h])
        h = step - 3
        if 0 <= h < CHUNKS:
            far2[h].wait_recv()
            if h == 0:
                for copy in w_loads:
                    copy.wait()
            block = lat[h].reshape(256, CHUNK)
            for e in range(3):
                part = lax.dot_general(
                    block, w[e, :, h * CHUNK : (h + 1) * CHUNK], (((1,), (1,)), ((), ())), preferred_element_type=F32
                )
                y_acc[e] = part if h == 0 else y_acc[e] + part

    s = lax.broadcasted_iota(jnp.int32, (1, 16, 192), 1) % 2
    first, second, third = (y_acc[e].reshape(PIECES, 16, 192) for e in range(3))
    edge = jnp.zeros((1, 16, 192), F32)
    from_left = jnp.concatenate([edge, pltpu.roll(first, 15, 1)[: PIECES - 1]], axis=0)
    from_right = jnp.concatenate([pltpu.roll(third, 1, 1)[1:], edge], axis=0)
    total = second + jnp.where(s == 1, pltpu.roll(first, 1, 1), from_left)
    total += jnp.where(s == 0, pltpu.roll(third, 15, 1), from_right)
    total = total.reshape(PIECES, 2, 8, 192)
    upper, lower = total[:, 0], total[:, 1]

    def pack(part):
        return jnp.concatenate([part[:8].reshape(64, OUT_DEV), part[8:].reshape(64, OUT_DEV)], axis=1)

    u_out[0] = pack(upper[..., 128:192])
    u_out[1] = pack(lower[..., 0:64])
    rows_sent = [
        send(u_out.at[0], u_in.at[1], u_send.at[0], u_recv.at[0], (up, col)),
        send(u_out.at[1], u_in.at[0], u_send.at[1], u_recv.at[1], (down, col)),
    ]
    load_mean.wait()
    centre = lat[col // 2, :, :, :, pl.ds(pl.multiple_of((col % 2) * CHANS, CHANS), CHANS)].reshape(256, CHANS)
    shortcut = jnp.dot(centre, g_mean[...], preferred_element_type=F32).reshape(PIECES, 2, 8, OUT_DEV)
    result0 = upper[..., 64:128] + lower[..., 128:192] + shortcut[:, 0]
    result1 = upper[..., 0:64] + lower[..., 64:128] + shortcut[:, 1]

    for copy in rows_sent:
        copy.wait_recv()

    def unpack(part, there):
        part = jnp.where(there, part, 0.0)
        return jnp.concatenate(
            [part[:, :OUT_DEV].reshape(8, 8, OUT_DEV), part[:, OUT_DEV:].reshape(8, 8, OUT_DEV)], axis=0
        )

    out_ref[0] = (result0 + unpack(u_in[0], has_up)).reshape(128, OUT_DEV).astype(BF16)
    out_ref[1] = (result1 + unpack(u_in[1], has_down)).reshape(128, OUT_DEV).astype(BF16)
    for copy in sent + pending + rows_sent:
        copy.wait_send()


def per_device(n_row, n_col, frames_in, norm_gain, first_kernel, second_kernel, latent_kernel):
    g_own, g_halo = spread_tables()
    anywhere = pl.BlockSpec(memory_space=pl.ANY)
    dma = pltpu.SemaphoreType.DMA
    out = pl.pallas_call(
        functools.partial(kernel, n_row, n_col),
        out_shape=jax.ShapeDtypeStruct((2, 128, OUT_DEV), BF16),
        in_specs=[anywhere] * 9,
        out_specs=pl.BlockSpec(memory_space=pltpu.VMEM),
        scratch_shapes=[
            pltpu.VMEM((4, 4, 16, CHANS), BF16),
            pltpu.VMEM((1, CHANS), F32),
            pltpu.VMEM((3, 3, 3, CHANS, CHANS), BF16),
            pltpu.VMEM((3, 3, 3, CHANS, CHANS), BF16),
            pltpu.VMEM((3, 3 * OUT_DEV, LATENT), BF16),
            pltpu.VMEM((1024, 256), BF16),
            pltpu.VMEM((1024, 384), BF16),
            pltpu.VMEM((128, 256), BF16),
            pltpu.VMEM((CHANS, OUT_DEV), BF16),
            pltpu.VMEM((2, 4, 16, CHANS), BF16),
            pltpu.VMEM((20, 16, CHANS), BF16),
            pltpu.VMEM((40, 16, CHANS), BF16),
            pltpu.VMEM((8, 8, 16, CHANS), BF16),
            pltpu.VMEM((6, 6, 16, CHANS), BF16),
            pltpu.VMEM((3, 576, CHANS), F32),
            pltpu.VMEM((CHUNKS, RING, RING, 16, CHUNK), BF16),
            pltpu.VMEM((3, 256, 3 * OUT_DEV), F32),
            pltpu.VMEM((2, 64, 2 * OUT_DEV), F32),
            pltpu.VMEM((2, 64, 2 * OUT_DEV), F32),
            pltpu.VMEM((256, CHANS), F32),
            dma((8,)),
            dma((9,)),
            dma((8,)),
            dma((8,)),
            dma((CHUNKS, 2)),
            dma((CHUNKS, 2)),
            dma((CHUNKS,)),
            dma((CHUNKS,)),
            dma((CHUNKS, 2)),
            dma((CHUNKS, 2)),
            dma((CHUNKS,)),
            dma((CHUNKS,)),
            dma((2,)),
            dma((2,)),
        ],
        compiler_params=pltpu.CompilerParams(
            collective_id=0, has_side_effects=True, vmem_limit_bytes=48 << 20
        ),
        cost_estimate=pl.CostEstimate(flops=4 << 30, bytes_accessed=14 << 20, transcendentals=1 << 18),
    )(
        frames_in.reshape(4, 4, 16, CHANS),
        norm_gain.reshape(1, CHANS),
        first_kernel,
        second_kernel,
        latent_kernel.transpose(0, 1, 3, 2),
        g_own,
        g_halo,
        strip_table(),
        mean_table(),
    )
    out = out.reshape(2, PIECES, FRAMES, 2, OUT_DEV)
    return out.transpose(2, 0, 1, 3, 4).reshape(FRAMES, 2, 2 * PIECES, OUT_DEV)


def solution(mesh):
    return jax.shard_map(
        functools.partial(per_device, mesh.shape["row"], mesh.shape["col"]),
        mesh=mesh,
        in_specs=(P(None, "row", "col", None), P(), P(), P(), P(None, None, None, "col")),
        out_specs=P(None, "row", None, "col"),
        check_vma=False,
    )
```

```python
import functools

import jax
import jax.numpy as jnp
import numpy as np
from jax import lax
from jax.experimental import pallas as pl
from jax.experimental.pallas import tpu as pltpu
from jax.sharding import PartitionSpec as P

MESH = pl.DeviceIdType.MESH
F32 = jnp.float32
BF16 = jnp.bfloat16
FRAMES, SIDE, CHANS = 4, 8, 256
OUT_CH, LATENT = 1024, 4096
RING = 4
PIECES = RING * RING
OUT_DEV = OUT_CH // PIECES
PARTS = ((0, 6, False), (6, 12, False), (12, 16, True))
CHUNKS = len(PARTS)
ORDER = """
    n0 n2 N00 n1 N10 f2 f0 N01 N03 f1 N11 N13 N20 N21 N23 N22
    F00 F10 N02 N12 F01 F03 F11 F13 F20 F21 F23 F22 F02 F12 W0 W1 W2
"""


def one_hot(index, width):
    out = np.zeros((len(index), width), np.float32)
    for at, source in enumerate(index):
        if source >= 0:
            out[at, source] = 1
    return out.astype(BF16)


def spread_tables():
    own, halo = [], []
    for p in range(-2, 6):
        for q in range(-2, 6):
            for i in range(2):
                for f in range(FRAMES):
                    for j in range(2):
                        r, c = 4 * i + p, 4 * j + q
                        inside_r, inside_c = 0 <= r < SIDE, 0 <= c < SIDE
                        a, b = -1, -1
                        side = 0 if c < 0 else 1
                        cc = c + 2 if c < 0 else c - SIDE
                        rr = r + 2 if r < 0 else r - SIDE
                        if inside_r and inside_c:
                            a = f * 64 + r * 8 + c
                        elif inside_c:
                            b = ((0 if r < 0 else 4) + f) * 16 + rr * 8 + c
                        elif inside_r:
                            b = (8 + 4 * side + r // 2) * 16 + f * 4 + (r % 2) * 2 + cc
                        else:
                            b = (16 + (0 if r < 0 else 2) + side) * 16 + f * 4 + rr * 2 + cc
                        own.append(a)
                        halo.append(b)
    return one_hot(own, 256), one_hot(halo, 384)


def strip_table():
    index = []
    for side in range(2):
        for rp in range(4):
            for f in range(FRAMES):
                for rr in range(2):
                    for cc in range(2):
                        index.append(f * 64 + (2 * rp + rr) * 8 + 6 * side + cc)
    return one_hot(index, 256)


def mean_table():
    group = LATENT // OUT_CH
    out = np.zeros((CHANS, CHANS // group), np.float32)
    out[np.arange(CHANS), np.arange(CHANS) // group] = 1 / group
    return out.astype(BF16)


def convolve(src, w, n, acc):
    rows = n * n * 16
    for a in range(3):
        total = None
        for b in range(3):
            for e in range(3):
                part = jnp.dot(src[b : b + n, e : e + n].reshape(rows, CHANS), w[a, b, e], preferred_element_type=F32)
                total = part if total is None else total + part
        acc[a, :rows] = total


def joined(acc, rows):
    early, same, late = (acc[a, :rows].reshape(rows // 8, 8, CHANS) for a in range(3))
    f = lax.broadcasted_iota(jnp.int32, (1, 8, CHANS), 1) // 2
    return same + jnp.where(f > 0, pltpu.roll(early, 2, 1), 0.0) + jnp.where(f < FRAMES - 1, pltpu.roll(late, 6, 1), 0.0)


def kernel(
    n_row, n_col,
    x_hbm, gain_hbm, k1_hbm, k2_hbm, w_hbm, g_own_hbm, g_halo_hbm, g_strip_hbm, g_mean_hbm,
    out_ref,
    x, gain, k1, k2, w, g_own, g_halo, g_strip, g_mean,
    strips, halo, normed, cells, hidden, acc, lat, y_acc, u_out, u_in, kept,
    load_sem, w_sem, halo_send, halo_recv,
    near_send, near_recv, far_send, far_recv, near2_send, near2_recv, far2_send, far2_recv,
    u_send, u_recv,
):
    row, col = lax.axis_index("row"), lax.axis_index("col")
    zh, y = col // RING, col % RING
    up, down = lax.rem(row + n_row - 1, n_row), lax.rem(row + 1, n_row)
    left, right = lax.rem(col + n_col - 1, n_col), lax.rem(col + 1, n_col)
    z_next, z_prev = lax.rem(zh + 1, RING), lax.rem(zh + RING - 1, RING)
    y_next, y_prev = lax.rem(y + 1, RING), lax.rem(y + RING - 1, RING)
    to_z = ((row, z_next * RING + y), (row, z_prev * RING + y))
    to_y = ((row, zh * RING + y_next), (row, zh * RING + y_prev))

    barrier = pltpu.get_barrier_semaphore()
    around = (
        (up, col), (down, col), (row, left), (row, right),
        (up, left), (up, right), (down, left), (down, right),
    ) + to_z + to_y
    for target in around:
        pl.semaphore_signal(barrier, inc=1, device_id=target, device_id_type=MESH)

    loads = []
    for at, (source, target) in enumerate((
        (x_hbm, x), (g_strip_hbm, g_strip), (gain_hbm, gain), (g_own_hbm, g_own), (g_halo_hbm, g_halo),
        (k1_hbm, k1), (k2_hbm, k2), (g_mean_hbm, g_mean),
    )):
        copy = pltpu.make_async_copy(source, target, load_sem.at[at])
        copy.start()
        loads.append(copy)
    w_loads = []
    for b in range(3):
        for e in range(3):
            copy = pltpu.make_async_copy(w_hbm.at[b, e], w.at[e, pl.ds(b * OUT_DEV, OUT_DEV)], w_sem.at[b * 3 + e])
            copy.start()
            w_loads.append(copy)
    load_x, load_strip, load_gain, load_own, load_halo, load_k1, load_k2, load_mean = loads

    def send(source, target, send_sem, recv_sem, device):
        copy = pltpu.make_async_remote_copy(
            src_ref=source, dst_ref=target, send_sem=send_sem, recv_sem=recv_sem, device_id=device, device_id_type=MESH
        )
        copy.start()
        return copy

    load_x.wait()
    pl.semaphore_wait(barrier, len(around))
    sent = [
        send(x.at[:, 0], halo.at[pl.ds(4, 4)], halo_send.at[0], halo_recv.at[0], (up, col)),
        send(x.at[:, 3], halo.at[pl.ds(0, 4)], halo_send.at[1], halo_recv.at[1], (down, col)),
    ]
    load_strip.wait()
    own = x[...].reshape(256, CHANS)
    strips[...] = jnp.dot(g_strip[...], own, preferred_element_type=F32).astype(BF16).reshape(2, 4, 16, CHANS)
    sent += [
        send(strips.at[0, 3], halo.at[17], halo_send.at[4], halo_recv.at[4], (down, left)),
        send(strips.at[1, 3], halo.at[16], halo_send.at[5], halo_recv.at[5], (down, right)),
        send(strips.at[0, 0], halo.at[19], halo_send.at[6], halo_recv.at[6], (up, left)),
        send(strips.at[1, 0], halo.at[18], halo_send.at[7], halo_recv.at[7], (up, right)),
        send(strips.at[0], halo.at[pl.ds(12, 4)], halo_send.at[2], halo_recv.at[2], (row, left)),
        send(strips.at[1], halo.at[pl.ds(8, 4)], halo_send.at[3], halo_recv.at[3], (row, right)),
    ]

    load_gain.wait()

    def norm(raw):
        values = raw.astype(F32)
        scale = lax.rsqrt(jnp.mean(values * values, axis=-1, keepdims=True) + 1e-06)
        return values * scale * gain[...]

    normed[0:16] = norm(own).astype(BF16).reshape(16, 16, CHANS)
    normed[36:40] = jnp.zeros((4, 16, CHANS), BF16)
    load_own.wait()
    middle = g_own[...].reshape(8, 8, 16, 256)[2:6, 2:6].reshape(256, 256)
    kept[...] = jnp.dot(middle, own, preferred_element_type=F32)

    for copy in sent:
        copy.wait_recv()
    has_up, has_down = row > 0, row < n_row - 1
    has_left, has_right = col > 0, col < n_col - 1
    for start, count, there in (
        (0, 4, has_up), (4, 4, has_down), (8, 4, has_left), (12, 4, has_right),
        (16, 1, has_up & has_left), (17, 1, has_up & has_right),
        (18, 1, has_down & has_left), (19, 1, has_down & has_right),
    ):
        values = norm(halo[start : start + count].reshape(count * 16, CHANS))
        values = values * jnp.where(there, 1.0, 0.0).astype(F32)
        normed[16 + start : 16 + start + count] = values.astype(BF16).reshape(count, 16, CHANS)
    load_halo.wait()
    spread = jnp.dot(g_own[...], normed[0:16].reshape(256, CHANS), preferred_element_type=F32)
    spread += jnp.dot(g_halo[...], normed[16:40].reshape(384, CHANS), preferred_element_type=F32)
    cells[...] = spread.astype(BF16).reshape(8, 8, 16, CHANS)

    load_k1.wait()
    convolve(cells, k1, 6, acc)
    value = joined(acc, 576)
    value = (value / (1.0 + jnp.exp(-value))).reshape(6, 6, 2, 8, CHANS)
    hidden[...] = value.astype(BF16).reshape(6, 6, 16, CHANS)
    place = lax.broadcasted_iota(jnp.int32, (1, 16, CHANS), 1)
    i_of, j_of = place // 8, place % 2
    none = jnp.zeros((), BF16)
    for edge, outside, there in ((0, i_of == 0, has_up), (5, i_of == 1, has_down)):
        keep = jnp.logical_or(jnp.logical_not(outside), there)
        hidden[edge] = jnp.where(keep, hidden[edge].astype(F32), 0.0).astype(BF16)
    for edge, outside, there in ((0, j_of == 0, has_left), (5, j_of == 1, has_right)):
        keep = jnp.logical_or(jnp.logical_not(outside), there)
        hidden[:, edge] = jnp.where(keep, hidden[:, edge].astype(F32), 0.0).astype(BF16)

    load_k2.wait()
    convolve(hidden, k2, 4, acc)
    mixed = (kept[...].reshape(32, 8, CHANS) + joined(acc, 256)).astype(BF16).reshape(16, 16, CHANS)
    for tile in range(PIECES):
        lat[tile, zh, y] = mixed[tile]

    zs = [zh] + [lax.rem(zh + step, RING) for step in (1, 2, 3)]
    ys = [y] + [lax.rem(y + step, RING) for step in (1, 2, 3)]
    pending = []
    near, far, near2, far2, took = {}, {}, {}, {}, []

    def pieces(c, u, v, part=None):
        first, last, y_first = PARTS[c]
        if part is not None:
            middle = (first + last) // 2
            first, last = (first, middle) if part == 0 else (middle, last)
        a, b = (zs[v], ys[u]) if y_first else (zs[u], ys[v])
        return lat.at[pl.ds(first, last - first), a, b]

    def pass_on(piece, send_sem, recv_sem, device):
        copy = send(piece, piece, send_sem, recv_sem, device)
        pending.append(copy)
        return copy

    for move in ORDER.split():
        what, c, u = move[0], int(move[1]), int(move[2:] or 0)
        rings = (to_y, to_z) if PARTS[c][2] else (to_z, to_y)
        if what == "n":
            near[c] = [
                pass_on(pieces(c, 0, 0), near_send.at[c, d], near_recv.at[c, d], rings[0][d]) for d in range(2)
            ]
        elif what == "f":
            for copy in near[c]:
                copy.wait_recv()
            far[c] = [
                pass_on(pieces(c, 3 - 2 * d, 0, d), far_send.at[c, d], far_recv.at[c, d], rings[0][d]) for d in range(2)
            ]
        elif what == "N":
            if u == 2:
                for copy in far[c]:
                    copy.wait_recv()
            near2[c, u] = [
                pass_on(pieces(c, u, 0), near2_send.at[c, u, d], near2_recv.at[c, u, d], rings[1][d]) for d in range(2)
            ]
        elif what == "F":
            for copy in near2[c, u]:
                copy.wait_recv()
            d = (0, 1, 1, 0)[u] if c % 2 == 0 else (1, 1, 0, 0)[u]
            far2[c, u] = pass_on(pieces(c, u, 3 - 2 * d), far2_send.at[c, u], far2_recv.at[c, u], rings[1][d])
        else:
            for u in range(RING):
                far2[c, u].wait_recv()
            if not took:
                for copy in w_loads:
                    copy.wait()
            first, last, _ = PARTS[c]
            for e in range(3):
                part = None if not took else y_acc[e]
                for tile in range(first, last):
                    term = lax.dot_general(
                        lat[tile].reshape(256, CHANS),
                        w[e, :, tile * CHANS : (tile + 1) * CHANS],
                        (((1,), (1,)), ((), ())),
                        preferred_element_type=F32,
                    )
                    part = term if part is None else part + term
                y_acc[e] = part
            took.append(c)

    s = lax.broadcasted_iota(jnp.int32, (1, 16, 192), 1) % 2
    first, second, third = (y_acc[e].reshape(PIECES, 16, 192) for e in range(3))
    edge = jnp.zeros((1, 16, 192), F32)
    from_left = jnp.concatenate([edge, pltpu.roll(first, 15, 1)[: PIECES - 1]], axis=0)
    from_right = jnp.concatenate([pltpu.roll(third, 1, 1)[1:], edge], axis=0)
    total = second + jnp.where(s == 1, pltpu.roll(first, 1, 1), from_left)
    total += jnp.where(s == 0, pltpu.roll(third, 15, 1), from_right)
    total = total.reshape(PIECES, 2, 8, 192)
    upper, lower = total[:, 0], total[:, 1]

    def pack(part):
        return jnp.concatenate([part[:8].reshape(64, OUT_DEV), part[8:].reshape(64, OUT_DEV)], axis=1)

    u_out[0] = pack(upper[..., 128:192])
    u_out[1] = pack(lower[..., 0:64])
    rows_sent = [
        send(u_out.at[0], u_in.at[1], u_send.at[0], u_recv.at[0], (up, col)),
        send(u_out.at[1], u_in.at[0], u_send.at[1], u_recv.at[1], (down, col)),
    ]
    load_mean.wait()
    centre = lat[col].reshape(256, CHANS)
    shortcut = jnp.dot(centre, g_mean[...], preferred_element_type=F32).reshape(PIECES, 2, 8, OUT_DEV)
    result0 = upper[..., 64:128] + lower[..., 128:192] + shortcut[:, 0]
    result1 = upper[..., 0:64] + lower[..., 64:128] + shortcut[:, 1]

    for copy in rows_sent:
        copy.wait_recv()

    def unpack(part, there):
        part = jnp.where(there, part, 0.0)
        return jnp.concatenate(
            [part[:, :OUT_DEV].reshape(8, 8, OUT_DEV), part[:, OUT_DEV:].reshape(8, 8, OUT_DEV)], axis=0
        )

    out_ref[0] = (result0 + unpack(u_in[0], has_up)).reshape(128, OUT_DEV).astype(BF16)
    out_ref[1] = (result1 + unpack(u_in[1], has_down)).reshape(128, OUT_DEV).astype(BF16)
    for copy in sent + pending + rows_sent:
        copy.wait_send()


def per_device(n_row, n_col, frames_in, norm_gain, first_kernel, second_kernel, latent_kernel):
    g_own, g_halo = spread_tables()
    anywhere = pl.BlockSpec(memory_space=pltpu.HBM)
    dma = pltpu.SemaphoreType.DMA
    out = pl.pallas_call(
        functools.partial(kernel, n_row, n_col),
        out_shape=jax.ShapeDtypeStruct((2, 128, OUT_DEV), BF16),
        in_specs=[anywhere] * 9,
        out_specs=pl.BlockSpec(memory_space=pltpu.VMEM),
        scratch_shapes=[
            pltpu.VMEM((4, 4, 16, CHANS), BF16),
            pltpu.VMEM((1, CHANS), F32),
            pltpu.VMEM((3, 3, 3, CHANS, CHANS), BF16),
            pltpu.VMEM((3, 3, 3, CHANS, CHANS), BF16),
            pltpu.VMEM((3, 3 * OUT_DEV, LATENT), BF16),
            pltpu.VMEM((1024, 256), BF16),
            pltpu.VMEM((1024, 384), BF16),
            pltpu.VMEM((128, 256), BF16),
            pltpu.VMEM((CHANS, OUT_DEV), BF16),
            pltpu.VMEM((2, 4, 16, CHANS), BF16),
            pltpu.VMEM((20, 16, CHANS), BF16),
            pltpu.VMEM((40, 16, CHANS), BF16),
            pltpu.VMEM((8, 8, 16, CHANS), BF16),
            pltpu.VMEM((6, 6, 16, CHANS), BF16),
            pltpu.VMEM((3, 576, CHANS), F32),
            pltpu.VMEM((PIECES, RING, RING, 16, CHANS), BF16),
            pltpu.VMEM((3, 256, 3 * OUT_DEV), F32),
            pltpu.VMEM((2, 64, 2 * OUT_DEV), F32),
            pltpu.VMEM((2, 64, 2 * OUT_DEV), F32),
            pltpu.VMEM((256, CHANS), F32),
            dma((8,)),
            dma((9,)),
            dma((8,)),
            dma((8,)),
            dma((CHUNKS, 2)),
            dma((CHUNKS, 2)),
            dma((CHUNKS, 2)),
            dma((CHUNKS, 2)),
            dma((CHUNKS, RING, 2)),
            dma((CHUNKS, RING, 2)),
            dma((CHUNKS, RING)),
            dma((CHUNKS, RING)),
            dma((2,)),
            dma((2,)),
        ],
        compiler_params=pltpu.CompilerParams(
            collective_id=0, has_side_effects=True, vmem_limit_bytes=60 << 20
        ),
        cost_estimate=pl.CostEstimate(flops=4 << 30, bytes_accessed=14 << 20, transcendentals=1 << 18),
    )(
        frames_in.reshape(4, 4, 16, CHANS),
        norm_gain.reshape(1, CHANS),
        first_kernel,
        second_kernel,
        latent_kernel.transpose(0, 1, 3, 2),
        g_own,
        g_halo,
        strip_table(),
        mean_table(),
    )
    out = out.reshape(2, PIECES, FRAMES, 2, OUT_DEV)
    return out.transpose(2, 0, 1, 3, 4).reshape(FRAMES, 2, 2 * PIECES, OUT_DEV)


def solution(mesh):
    return jax.shard_map(
        functools.partial(per_device, mesh.shape["row"], mesh.shape["col"]),
        mesh=mesh,
        in_specs=(P(None, "row", "col", None), P(), P(), P(), P(None, None, None, "col")),
        out_specs=P(None, "row", None, "col"),
        check_vma=False,
    )
```

```python
import functools

import jax
import jax.numpy as jnp
import numpy as np
from jax import lax
from jax.experimental import pallas as pl
from jax.experimental.pallas import tpu as pltpu
from jax.sharding import PartitionSpec as P

MESH = pl.DeviceIdType.MESH
F32 = jnp.float32
BF16 = jnp.bfloat16
FRAMES, SIDE, CHANS = 4, 8, 256
OUT_CH, LATENT = 1024, 4096
RING = 4
PIECES = RING * RING
OUT_DEV = OUT_CH // PIECES
PARTS = ((0, 6, False), (6, 12, False), (12, 16, True))
CHUNKS = len(PARTS)
ORDER = (
    ("n0", "n2", "N00", "n1", "N10", "f2", "f0", "N01", "N03", "f1", "N11", "N13", "N20", "N21", "N23", "N22")
    + ("F00", "F10", "N02", "N12", "F01", "F03", "F11", "F13", "F20", "F21", "F02", "F12", "F23", "F22", "W0", "W1", "W2")
)


def one_hot(index, width):
    out = np.zeros((len(index), width), np.float32)
    for at, source in enumerate(index):
        if source >= 0:
            out[at, source] = 1
    return out.astype(BF16)


OWN_TILES = [(p, q) for p in range(1, 5) for q in range(1, 5)]
OTHER_TILES = [(p, q) for p in range(9) for q in range(9) if (p, q) not in OWN_TILES]


def line_of(tile, half):
    if tile < 6:
        return 4 * half + tile - 1
    return tile - 6 + (7 if half else -2)


def spread_tables():
    own, halo = [], []
    for p, q in OWN_TILES + OTHER_TILES:
        for i in range(2):
            for f in range(FRAMES):
                for j in range(2):
                    r, c = line_of(p, i), line_of(q, j)
                    inside_r, inside_c = 0 <= r < SIDE, 0 <= c < SIDE
                    a, b = -1, -1
                    side = 0 if c < 0 else 1
                    cc = c + 2 if c < 0 else c - SIDE
                    rr = r + 2 if r < 0 else r - SIDE
                    if inside_r and inside_c:
                        a = f * 64 + r * 8 + c
                    elif inside_c:
                        b = ((0 if r < 0 else 4) + f) * 16 + rr * 8 + c
                    elif inside_r:
                        b = (8 + 4 * side + r // 2) * 16 + f * 4 + (r % 2) * 2 + cc
                    else:
                        b = (16 + (0 if r < 0 else 2) + side) * 16 + f * 4 + rr * 2 + cc
                    own.append(a)
                    halo.append(b)
    return one_hot(own, 256), one_hot(halo[256:], 384)


def strip_table():
    index = []
    for side in range(2):
        for rp in range(4):
            for f in range(FRAMES):
                for rr in range(2):
                    for cc in range(2):
                        index.append(f * 64 + (2 * rp + rr) * 8 + 6 * side + cc)
    return one_hot(index, 256)


def mean_table():
    group = LATENT // OUT_CH
    out = np.zeros((CHANS, CHANS // group), np.float32)
    out[np.arange(CHANS), np.arange(CHANS) // group] = 1 / group
    return out.astype(BF16)


def convolve_own(cells, w, acc):
    order = [(1, 1)] + [(b, e) for b in range(3) for e in range(3) if (b, e) != (1, 1)]
    for a in range(3):
        for b, e in order:
            p0, p1, q0, q1 = max(0, 1 - b), min(4, 5 - b), max(0, 1 - e), min(4, 5 - e)
            shape = (p1 - p0, q1 - q0, 16, CHANS)
            lhs = cells[p0 + b : p1 + b, q0 + e : q1 + e].reshape(-1, CHANS)
            part = jnp.dot(lhs, w[a, b, e], preferred_element_type=F32).reshape(shape)
            if (b, e) == (1, 1):
                acc[a, 0:4, 0:4] = part
            else:
                acc[a, p0:p1, q0:q1] += part


def convolve_rest(cells, w, acc):
    for a in range(3):
        for b in range(3):
            for e in range(3):
                tiles = [
                    (p, q) for p in range(5) for q in range(5)
                    if p == 4 or q == 4 or not (1 <= p + b <= 4 and 1 <= q + e <= 4)
                ]
                lhs = jnp.concatenate(
                    [cells[p + b if p < 4 else 6 + b, q + e if q < 4 else 6 + e] for p, q in tiles], axis=0
                )
                part = jnp.dot(lhs, w[a, b, e], preferred_element_type=F32)
                for at, (p, q) in enumerate(tiles):
                    term = part[at * 16 : (at + 1) * 16]
                    if (p == 4 or q == 4) and b == 0 and e == 0:
                        acc[a, p, q] = term
                    else:
                        acc[a, p, q] += term


def convolve(src, w, acc):
    for a in range(3):
        total = None
        for b in range(3):
            for e in range(3):
                part = jnp.dot(src[b : b + 4, e : e + 4].reshape(256, CHANS), w[a, b, e], preferred_element_type=F32)
                total = part if total is None else total + part
        acc[a, 0:4, 0:4] = total.reshape(4, 4, 16, CHANS)


def joined(acc, n):
    early, same, late = (acc[a, 0:n, 0:n].reshape(n * n * 2, 8, CHANS) for a in range(3))
    f = lax.broadcasted_iota(jnp.int32, (1, 8, CHANS), 1) // 2
    total = same + jnp.where(f > 0, pltpu.roll(early, 2, 1), 0.0)
    total += jnp.where(f < FRAMES - 1, pltpu.roll(late, 6, 1), 0.0)
    return total.reshape(n, n, 2, 8, CHANS)


def kernel(
    n_row, n_col,
    x_hbm, gain_hbm, k1_hbm, k2_hbm, w_hbm, g_own_hbm, g_halo_hbm, g_strip_hbm, g_mean_hbm,
    out_ref,
    x, gain, k1, k2, w, g_own, g_halo, g_strip, g_mean,
    strips, halo, normed, cells, others, hidden, acc, lat, y_acc, u_out, u_in, kept,
    load_sem, w_sem, halo_send, halo_recv,
    near_send, near_recv, far_send, far_recv, near2_send, near2_recv, far2_send, far2_recv,
    u_send, u_recv,
):
    row, col = lax.axis_index("row"), lax.axis_index("col")
    zh, y = col // RING, col % RING
    up, down = lax.rem(row + n_row - 1, n_row), lax.rem(row + 1, n_row)
    left, right = lax.rem(col + n_col - 1, n_col), lax.rem(col + 1, n_col)
    z_next, z_prev = lax.rem(zh + 1, RING), lax.rem(zh + RING - 1, RING)
    y_next, y_prev = lax.rem(y + 1, RING), lax.rem(y + RING - 1, RING)
    to_z = ((row, z_next * RING + y), (row, z_prev * RING + y))
    to_y = ((row, zh * RING + y_next), (row, zh * RING + y_prev))

    barrier = pltpu.get_barrier_semaphore()
    around = (
        (up, col), (down, col), (row, left), (row, right),
        (up, left), (up, right), (down, left), (down, right),
    ) + to_z + to_y
    for target in around:
        pl.semaphore_signal(barrier, inc=1, device_id=target, device_id_type=MESH)

    loads = []
    for at, (source, target) in enumerate((
        (x_hbm, x), (g_strip_hbm, g_strip), (gain_hbm, gain), (g_own_hbm, g_own), (k1_hbm, k1),
        (g_halo_hbm, g_halo), (k2_hbm, k2), (g_mean_hbm, g_mean),
    )):
        copy = pltpu.make_async_copy(source, target, load_sem.at[at])
        copy.start()
        loads.append(copy)
    w_loads = []
    for b in range(3):
        for e in range(3):
            copy = pltpu.make_async_copy(w_hbm.at[b, e], w.at[e, pl.ds(b * OUT_DEV, OUT_DEV)], w_sem.at[b * 3 + e])
            copy.start()
            w_loads.append(copy)
    load_x, load_strip, load_gain, load_own, load_k1, load_halo, load_k2, load_mean = loads

    def send(source, target, send_sem, recv_sem, device):
        copy = pltpu.make_async_remote_copy(
            src_ref=source, dst_ref=target, send_sem=send_sem, recv_sem=recv_sem, device_id=device, device_id_type=MESH
        )
        copy.start()
        return copy

    load_x.wait()
    load_strip.wait()
    own = x[...].reshape(256, CHANS)
    strips[...] = jnp.dot(g_strip[...], own, preferred_element_type=F32).astype(BF16).reshape(2, 4, 16, CHANS)
    pl.semaphore_wait(barrier, len(around))
    sent = [
        send(strips.at[0, 3], halo.at[17], halo_send.at[4], halo_recv.at[4], (down, left)),
        send(strips.at[1, 3], halo.at[16], halo_send.at[5], halo_recv.at[5], (down, right)),
        send(strips.at[0, 0], halo.at[19], halo_send.at[6], halo_recv.at[6], (up, left)),
        send(strips.at[1, 0], halo.at[18], halo_send.at[7], halo_recv.at[7], (up, right)),
        send(x.at[:, 0], halo.at[pl.ds(4, 4)], halo_send.at[0], halo_recv.at[0], (up, col)),
        send(x.at[:, 3], halo.at[pl.ds(0, 4)], halo_send.at[1], halo_recv.at[1], (down, col)),
        send(strips.at[0], halo.at[pl.ds(12, 4)], halo_send.at[2], halo_recv.at[2], (row, left)),
        send(strips.at[1], halo.at[pl.ds(8, 4)], halo_send.at[3], halo_recv.at[3], (row, right)),
    ]

    load_gain.wait()

    def norm(raw):
        values = raw.astype(F32)
        scale = lax.rsqrt(jnp.mean(values * values, axis=-1, keepdims=True) + 1e-06)
        return values * scale * gain[...]

    own_normed = norm(own).astype(BF16)
    normed[20:24] = jnp.zeros((4, 16, CHANS), BF16)
    load_own.wait()
    middle = jnp.dot(g_own[0:256], own_normed, preferred_element_type=F32)
    cells[1:5, 1:5] = middle.astype(BF16).reshape(4, 4, 16, CHANS)
    load_k1.wait()
    convolve_own(cells, k1, acc)
    others[...] = jnp.dot(g_own[256:], own_normed, preferred_element_type=F32)
    kept[...] = jnp.dot(g_own[0:256], own, preferred_element_type=F32)
    load_halo.wait()

    for copy in sent:
        copy.wait_recv()
    has_up, has_down = row > 0, row < n_row - 1
    has_left, has_right = col > 0, col < n_col - 1
    for start, count, there in (
        (0, 4, has_up), (4, 4, has_down), (8, 4, has_left), (12, 4, has_right),
        (16, 1, has_up & has_left), (17, 1, has_up & has_right),
        (18, 1, has_down & has_left), (19, 1, has_down & has_right),
    ):
        values = norm(halo[start : start + count].reshape(count * 16, CHANS))
        values = values * jnp.where(there, 1.0, 0.0).astype(F32)
        normed[start : start + count] = values.astype(BF16).reshape(count, 16, CHANS)
    spread = others[...] + jnp.dot(g_halo[...], normed[...].reshape(384, CHANS), preferred_element_type=F32)
    for at, (p, q) in enumerate(OTHER_TILES):
        cells[p, q] = spread[at * 16 : (at + 1) * 16].astype(BF16)

    convolve_rest(cells, k1, acc)
    value = joined(acc, 5)
    value = value / (1.0 + jnp.exp(-value))
    def flag(there):
        return jnp.where(there, 1.0, 0.0).astype(F32)

    j_of = lax.broadcasted_iota(jnp.int32, (1, 8, CHANS), 1) % 2
    sides = jnp.where(j_of == 0, flag(has_left), flag(has_right))
    inner, below = value[0:4], value[4]
    top = jnp.stack([below[:, 0] * flag(has_up), inner[3][:, 0]], axis=1)
    bottom = jnp.stack([inner[0][:, 1], below[:, 1] * flag(has_down)], axis=1)
    for p, line in enumerate((top, inner[0], inner[1], inner[2], inner[3], bottom)):
        edge = line[4] * sides
        first = jnp.where(j_of == 0, edge, pltpu.roll(line[3], 1, 1))
        last = jnp.where(j_of == 1, edge, pltpu.roll(line[0], 7, 1))
        for q, tile in enumerate((first, line[0], line[1], line[2], line[3], last)):
            hidden[p, q] = tile.reshape(16, CHANS).astype(BF16)

    load_k2.wait()
    convolve(hidden, k2, acc)
    mixed = (kept[...].reshape(4, 4, 2, 8, CHANS) + joined(acc, 4)).astype(BF16).reshape(16, 16, CHANS)
    for tile in range(PIECES):
        lat[tile, zh, y] = mixed[tile]

    zs = [zh] + [lax.rem(zh + step, RING) for step in (1, 2, 3)]
    ys = [y] + [lax.rem(y + step, RING) for step in (1, 2, 3)]
    pending = []
    near, far, near2, far2, took = {}, {}, {}, {}, []

    def pieces(c, u, v, part=None):
        first, last, y_first = PARTS[c]
        if part is not None:
            middle = (first + last) // 2
            first, last = (first, middle) if part == 0 else (middle, last)
        a, b = (zs[v], ys[u]) if y_first else (zs[u], ys[v])
        return lat.at[pl.ds(first, last - first), a, b]

    def pass_on(piece, send_sem, recv_sem, device):
        copy = send(piece, piece, send_sem, recv_sem, device)
        pending.append(copy)
        return copy

    for move in ORDER:
        what, c, u = move[0], int(move[1]), int(move[2:] or 0)
        rings = (to_y, to_z) if PARTS[c][2] else (to_z, to_y)
        if what == "n":
            near[c] = [
                pass_on(pieces(c, 0, 0), near_send.at[c, d], near_recv.at[c, d], rings[0][d]) for d in range(2)
            ]
        elif what == "f":
            for copy in near[c]:
                copy.wait_recv()
            far[c] = [
                pass_on(pieces(c, 3 - 2 * d, 0, d), far_send.at[c, d], far_recv.at[c, d], rings[0][d]) for d in range(2)
            ]
        elif what == "N":
            if u == 2:
                for copy in far[c]:
                    copy.wait_recv()
            near2[c, u] = [
                pass_on(pieces(c, u, 0), near2_send.at[c, u, d], near2_recv.at[c, u, d], rings[1][d]) for d in range(2)
            ]
        elif what == "F":
            for copy in near2[c, u]:
                copy.wait_recv()
            d = (0, 1, 1, 0)[u] if c % 2 == 0 else (1, 1, 0, 0)[u]
            far2[c, u] = pass_on(pieces(c, u, 3 - 2 * d), far2_send.at[c, u], far2_recv.at[c, u], rings[1][d])
        else:
            for u in range(RING):
                far2[c, u].wait_recv()
            if not took:
                for copy in w_loads:
                    copy.wait()
            first, last, _ = PARTS[c]
            for e in range(3):
                part = None if not took else y_acc[e]
                for tile in range(first, last):
                    term = lax.dot_general(
                        lat[tile].reshape(256, CHANS),
                        w[e, :, tile * CHANS : (tile + 1) * CHANS],
                        (((1,), (1,)), ((), ())),
                        preferred_element_type=F32,
                    )
                    part = term if part is None else part + term
                y_acc[e] = part
            took.append(c)

    s = lax.broadcasted_iota(jnp.int32, (1, 16, 192), 1) % 2
    first, second, third = (y_acc[e].reshape(PIECES, 16, 192) for e in range(3))
    edge = jnp.zeros((1, 16, 192), F32)
    from_left = jnp.concatenate([edge, pltpu.roll(first, 15, 1)[: PIECES - 1]], axis=0)
    from_right = jnp.concatenate([pltpu.roll(third, 1, 1)[1:], edge], axis=0)
    total = second + jnp.where(s == 1, pltpu.roll(first, 1, 1), from_left)
    total += jnp.where(s == 0, pltpu.roll(third, 15, 1), from_right)
    total = total.reshape(PIECES, 2, 8, 192)
    upper, lower = total[:, 0], total[:, 1]

    def pack(part):
        return jnp.concatenate([part[:8].reshape(64, OUT_DEV), part[8:].reshape(64, OUT_DEV)], axis=1)

    u_out[0] = pack(upper[..., 128:192])
    u_out[1] = pack(lower[..., 0:64])
    rows_sent = [
        send(u_out.at[0], u_in.at[1], u_send.at[0], u_recv.at[0], (up, col)),
        send(u_out.at[1], u_in.at[0], u_send.at[1], u_recv.at[1], (down, col)),
    ]
    load_mean.wait()
    centre = lat[col].reshape(256, CHANS)
    shortcut = jnp.dot(centre, g_mean[...], preferred_element_type=F32).reshape(PIECES, 2, 8, OUT_DEV)
    result0 = upper[..., 64:128] + lower[..., 128:192] + shortcut[:, 0]
    result1 = upper[..., 0:64] + lower[..., 64:128] + shortcut[:, 1]

    for copy in rows_sent:
        copy.wait_recv()

    def unpack(part, there):
        part = jnp.where(there, part, 0.0)
        return jnp.concatenate(
            [part[:, :OUT_DEV].reshape(8, 8, OUT_DEV), part[:, OUT_DEV:].reshape(8, 8, OUT_DEV)], axis=0
        )

    out_ref[0] = (result0 + unpack(u_in[0], has_up)).reshape(128, OUT_DEV).astype(BF16)
    out_ref[1] = (result1 + unpack(u_in[1], has_down)).reshape(128, OUT_DEV).astype(BF16)
    for copy in sent + pending + rows_sent:
        copy.wait_send()


def per_device(n_row, n_col, frames_in, norm_gain, first_kernel, second_kernel, latent_kernel):
    g_own, g_halo = spread_tables()
    anywhere = pl.BlockSpec(memory_space=pltpu.HBM)
    dma = pltpu.SemaphoreType.DMA
    out = pl.pallas_call(
        functools.partial(kernel, n_row, n_col),
        out_shape=jax.ShapeDtypeStruct((2, 128, OUT_DEV), BF16),
        in_specs=[anywhere] * 9,
        out_specs=pl.BlockSpec(memory_space=pltpu.VMEM),
        scratch_shapes=[
            pltpu.VMEM((4, 4, 16, CHANS), BF16),
            pltpu.VMEM((1, CHANS), F32),
            pltpu.VMEM((3, 3, 3, CHANS, CHANS), BF16),
            pltpu.VMEM((3, 3, 3, CHANS, CHANS), BF16),
            pltpu.VMEM((3, 3 * OUT_DEV, LATENT), BF16),
            pltpu.VMEM((81 * 16, 256), BF16),
            pltpu.VMEM((65 * 16, 384), BF16),
            pltpu.VMEM((128, 256), BF16),
            pltpu.VMEM((CHANS, OUT_DEV), BF16),
            pltpu.VMEM((2, 4, 16, CHANS), BF16),
            pltpu.VMEM((20, 16, CHANS), BF16),
            pltpu.VMEM((24, 16, CHANS), BF16),
            pltpu.VMEM((9, 9, 16, CHANS), BF16),
            pltpu.VMEM((65 * 16, CHANS), F32),
            pltpu.VMEM((6, 6, 16, CHANS), BF16),
            pltpu.VMEM((3, 5, 5, 16, CHANS), F32),
            pltpu.VMEM((PIECES, RING, RING, 16, CHANS), BF16),
            pltpu.VMEM((3, 256, 3 * OUT_DEV), F32),
            pltpu.VMEM((2, 64, 2 * OUT_DEV), F32),
            pltpu.VMEM((2, 64, 2 * OUT_DEV), F32),
            pltpu.VMEM((256, CHANS), F32),
            dma((8,)),
            dma((9,)),
            dma((8,)),
            dma((8,)),
            dma((CHUNKS, 2)),
            dma((CHUNKS, 2)),
            dma((CHUNKS, 2)),
            dma((CHUNKS, 2)),
            dma((CHUNKS, RING, 2)),
            dma((CHUNKS, RING, 2)),
            dma((CHUNKS, RING)),
            dma((CHUNKS, RING)),
            dma((2,)),
            dma((2,)),
        ],
        compiler_params=pltpu.CompilerParams(
            collective_id=0, has_side_effects=True, vmem_limit_bytes=60 << 20
        ),
        cost_estimate=pl.CostEstimate(flops=4 << 30, bytes_accessed=14 << 20, transcendentals=1 << 18),
    )(
        frames_in.reshape(4, 4, 16, CHANS),
        norm_gain.reshape(1, CHANS),
        first_kernel,
        second_kernel,
        latent_kernel.transpose(0, 1, 3, 2),
        g_own,
        g_halo,
        strip_table(),
        mean_table(),
    )
    out = out.reshape(2, PIECES, FRAMES, 2, OUT_DEV)
    return out.transpose(2, 0, 1, 3, 4).reshape(FRAMES, 2, 2 * PIECES, OUT_DEV)


def solution(mesh):
    return jax.shard_map(
        functools.partial(per_device, mesh.shape["row"], mesh.shape["col"]),
        mesh=mesh,
        in_specs=(P(None, "row", "col", None), P(), P(), P(), P(None, None, None, "col")),
        out_specs=P(None, "row", None, "col"),
        check_vma=False,
    )
```

```python
import functools

import jax
import jax.numpy as jnp
import numpy as np
from jax import lax
from jax.experimental import pallas as pl
from jax.experimental.pallas import tpu as pltpu
from jax.sharding import PartitionSpec as P

MESH = pl.DeviceIdType.MESH
F32 = jnp.float32
BF16 = jnp.bfloat16
FRAMES, SIDE, CHANS = 4, 8, 256
OUT_CH, LATENT = 1024, 4096
RING = 4
PIECES = RING * RING
OUT_DEV = OUT_CH // PIECES
PARTS = ((0, 6, False), (6, 12, False), (12, 16, True))
CHUNKS = len(PARTS)
ORDER = (
    ("C0", "C1", "n0", "n2", "d2", "N00", "n1", "N10", "e2", "f0", "N01", "N03", "f1", "N11", "N13", "N20", "N21", "N23", "N22")
    + ("F00", "F10", "D02", "D12", "F01", "F03", "F11", "F13", "F20", "F21", "F23", "F22", "W00132", "W10132", "W20132")
)


def one_hot(index, width):
    out = np.zeros((len(index), width), np.float32)
    for at, source in enumerate(index):
        if source >= 0:
            out[at, source] = 1
    return out.astype(BF16)


OWN_TILES = [(p, q) for p in range(1, 5) for q in range(1, 5)]
OTHER_TILES = [(p, q) for p in range(9) for q in range(9) if (p, q) not in OWN_TILES]


def line_of(tile, half):
    if tile < 6:
        return 4 * half + tile - 1
    return tile - 6 + (7 if half else -2)


def spread_tables():
    own, halo = [], []
    for p, q in OWN_TILES + OTHER_TILES:
        for i in range(2):
            for f in range(FRAMES):
                for j in range(2):
                    r, c = line_of(p, i), line_of(q, j)
                    inside_r, inside_c = 0 <= r < SIDE, 0 <= c < SIDE
                    a, b = -1, -1
                    side = 0 if c < 0 else 1
                    cc = c + 2 if c < 0 else c - SIDE
                    rr = r + 2 if r < 0 else r - SIDE
                    if inside_r and inside_c:
                        a = f * 64 + r * 8 + c
                    elif inside_c:
                        b = ((0 if r < 0 else 4) + f) * 16 + rr * 8 + c
                    elif inside_r:
                        b = (8 + 4 * side + r // 2) * 16 + f * 4 + (r % 2) * 2 + cc
                    else:
                        b = (16 + (0 if r < 0 else 2) + side) * 16 + f * 4 + rr * 2 + cc
                    own.append(a)
                    halo.append(b)
    return one_hot(own, 256), one_hot(halo[256:], 384)


def strip_table():
    index = []
    for side in range(2):
        for rp in range(4):
            for f in range(FRAMES):
                for rr in range(2):
                    for cc in range(2):
                        index.append(f * 64 + (2 * rp + rr) * 8 + 6 * side + cc)
    return one_hot(index, 256)


def mean_table():
    group = LATENT // OUT_CH
    out = np.zeros((CHANS, CHANS // group), np.float32)
    out[np.arange(CHANS), np.arange(CHANS) // group] = 1 / group
    return out.astype(BF16)


def convolve_own(cells, w, acc):
    order = [(1, 1)] + [(b, e) for b in range(3) for e in range(3) if (b, e) != (1, 1)]
    for a in range(3):
        for b, e in order:
            p0, p1, q0, q1 = max(0, 1 - b), min(4, 5 - b), max(0, 1 - e), min(4, 5 - e)
            shape = (p1 - p0, q1 - q0, 16, CHANS)
            lhs = cells[p0 + b : p1 + b, q0 + e : q1 + e].reshape(-1, CHANS)
            part = jnp.dot(lhs, w[a, b, e], preferred_element_type=F32).reshape(shape)
            if (b, e) == (1, 1):
                acc[a, 0:4, 0:4] = part
            else:
                acc[a, p0:p1, q0:q1] += part


def convolve_rest(cells, w, acc):
    for a in range(3):
        for b in range(3):
            for e in range(3):
                tiles = [
                    (p, q) for p in range(5) for q in range(5)
                    if p == 4 or q == 4 or not (1 <= p + b <= 4 and 1 <= q + e <= 4)
                ]
                lhs = jnp.concatenate(
                    [cells[p + b if p < 4 else 6 + b, q + e if q < 4 else 6 + e] for p, q in tiles], axis=0
                )
                part = jnp.dot(lhs, w[a, b, e], preferred_element_type=F32)
                for at, (p, q) in enumerate(tiles):
                    term = part[at * 16 : (at + 1) * 16]
                    if (p == 4 or q == 4) and b == 0 and e == 0:
                        acc[a, p, q] = term
                    else:
                        acc[a, p, q] += term


def convolve(src, w, acc, half):
    for a in range(3):
        total = None
        for b in range(3):
            for e in range(3):
                lhs = src[2 * half + b : 2 * half + b + 2, e : e + 4].reshape(128, CHANS)
                part = jnp.dot(lhs, w[a, b, e], preferred_element_type=F32)
                total = part if total is None else total + part
        acc[a, 0:2, 0:4] = total.reshape(2, 4, 16, CHANS)


def joined(acc, m, n):
    early, same, late = (acc[a, 0:m, 0:n].reshape(m * n * 2, 8, CHANS) for a in range(3))
    f = lax.broadcasted_iota(jnp.int32, (1, 8, CHANS), 1) // 2
    total = same + jnp.where(f > 0, pltpu.roll(early, 2, 1), 0.0)
    total += jnp.where(f < FRAMES - 1, pltpu.roll(late, 6, 1), 0.0)
    return total.reshape(m, n, 2, 8, CHANS)


def kernel(
    n_row, n_col,
    x_hbm, gain_hbm, k1_hbm, k2_hbm, w_hbm, g_own_hbm, g_halo_hbm, g_strip_hbm, g_mean_hbm,
    out_ref,
    x, gain, k1, k2, w, g_own, g_halo, g_strip, g_mean,
    strips, halo, normed, cells, others, hidden, acc, lat, y_acc, u_out, u_in, kept,
    load_sem, w_sem, halo_send, halo_recv,
    near_send, near_recv, far_send, far_recv, near2_send, near2_recv, far2_send, far2_recv,
    u_send, u_recv,
):
    row, col = lax.axis_index("row"), lax.axis_index("col")
    zh, y = col // RING, col % RING
    up, down = lax.rem(row + n_row - 1, n_row), lax.rem(row + 1, n_row)
    left, right = lax.rem(col + n_col - 1, n_col), lax.rem(col + 1, n_col)
    z_next, z_prev = lax.rem(zh + 1, RING), lax.rem(zh + RING - 1, RING)
    y_next, y_prev = lax.rem(y + 1, RING), lax.rem(y + RING - 1, RING)
    to_z = ((row, z_next * RING + y), (row, z_prev * RING + y))
    to_y = ((row, zh * RING + y_next), (row, zh * RING + y_prev))

    to_z2 = (row, lax.rem(zh + 2, RING) * RING + y)
    to_y2 = (row, zh * RING + lax.rem(y + 2, RING))

    barrier = pltpu.get_barrier_semaphore()
    around = (
        (up, col), (down, col), (row, left), (row, right),
        (up, left), (up, right), (down, left), (down, right),
    ) + to_z + to_y + (to_z2, to_y2)
    for target in around:
        pl.semaphore_signal(barrier, inc=1, device_id=target, device_id_type=MESH)

    loads = []
    for at, (source, target) in enumerate((
        (x_hbm, x), (g_strip_hbm, g_strip), (gain_hbm, gain), (g_own_hbm, g_own), (k1_hbm, k1),
        (g_halo_hbm, g_halo), (k2_hbm, k2), (g_mean_hbm, g_mean),
    )):
        copy = pltpu.make_async_copy(source, target, load_sem.at[at])
        copy.start()
        loads.append(copy)
    w_loads = []
    for b in range(3):
        copy = pltpu.make_async_copy(w_hbm.at[b], w.at[b], w_sem.at[b])
        copy.start()
        w_loads.append(copy)
    load_x, load_strip, load_gain, load_own, load_k1, load_halo, load_k2, load_mean = loads

    def send(source, target, send_sem, recv_sem, device):
        copy = pltpu.make_async_remote_copy(
            src_ref=source, dst_ref=target, send_sem=send_sem, recv_sem=recv_sem, device_id=device, device_id_type=MESH
        )
        copy.start()
        return copy

    load_x.wait()
    load_strip.wait()
    own = x[...].reshape(256, CHANS)
    strips[...] = jnp.dot(g_strip[...], own, preferred_element_type=F32).astype(BF16).reshape(2, 4, 16, CHANS)
    pl.semaphore_wait(barrier, len(around))
    sent = [
        send(strips.at[0, 3], halo.at[17], halo_send.at[4], halo_recv.at[4], (down, left)),
        send(strips.at[1, 3], halo.at[16], halo_send.at[5], halo_recv.at[5], (down, right)),
        send(strips.at[0, 0], halo.at[19], halo_send.at[6], halo_recv.at[6], (up, left)),
        send(strips.at[1, 0], halo.at[18], halo_send.at[7], halo_recv.at[7], (up, right)),
        send(x.at[:, 0], halo.at[pl.ds(4, 4)], halo_send.at[0], halo_recv.at[0], (up, col)),
        send(x.at[:, 3], halo.at[pl.ds(0, 4)], halo_send.at[1], halo_recv.at[1], (down, col)),
        send(strips.at[0], halo.at[pl.ds(12, 4)], halo_send.at[2], halo_recv.at[2], (row, left)),
        send(strips.at[1], halo.at[pl.ds(8, 4)], halo_send.at[3], halo_recv.at[3], (row, right)),
    ]

    load_gain.wait()

    def norm(raw):
        values = raw.astype(F32)
        scale = lax.rsqrt(jnp.mean(values * values, axis=-1, keepdims=True) + 1e-06)
        return values * scale * gain[...]

    own_normed = norm(own).astype(BF16)
    normed[20:24] = jnp.zeros((4, 16, CHANS), BF16)
    y_acc[...] = jnp.zeros(y_acc.shape, F32)
    load_own.wait()
    middle = jnp.dot(g_own[0:256], own_normed, preferred_element_type=F32)
    cells[1:5, 1:5] = middle.astype(BF16).reshape(4, 4, 16, CHANS)
    load_k1.wait()
    convolve_own(cells, k1, acc)
    others[...] = jnp.dot(g_own[256:], own_normed, preferred_element_type=F32)
    kept[...] = jnp.dot(g_own[0:256], own, preferred_element_type=F32)
    load_halo.wait()

    for copy in sent:
        copy.wait_recv()
    has_up, has_down = row > 0, row < n_row - 1
    has_left, has_right = col > 0, col < n_col - 1
    for start, count, there in (
        (0, 4, has_up), (4, 4, has_down), (8, 4, has_left), (12, 4, has_right),
        (16, 1, has_up & has_left), (17, 1, has_up & has_right),
        (18, 1, has_down & has_left), (19, 1, has_down & has_right),
    ):
        values = norm(halo[start : start + count].reshape(count * 16, CHANS))
        values = values * jnp.where(there, 1.0, 0.0).astype(F32)
        normed[start : start + count] = values.astype(BF16).reshape(count, 16, CHANS)
    spread = others[...] + jnp.dot(g_halo[...], normed[...].reshape(384, CHANS), preferred_element_type=F32)
    for at, (p, q) in enumerate(OTHER_TILES):
        cells[p, q] = spread[at * 16 : (at + 1) * 16].astype(BF16)

    convolve_rest(cells, k1, acc)
    value = joined(acc, 5, 5)
    value = value / (1.0 + jnp.exp(-value))
    def flag(there):
        return jnp.where(there, 1.0, 0.0).astype(F32)

    j_of = lax.broadcasted_iota(jnp.int32, (1, 8, CHANS), 1) % 2
    sides = jnp.where(j_of == 0, flag(has_left), flag(has_right))
    inner, below = value[0:4], value[4]
    top = jnp.stack([below[:, 0] * flag(has_up), inner[3][:, 0]], axis=1)
    bottom = jnp.stack([inner[0][:, 1], below[:, 1] * flag(has_down)], axis=1)
    for p, line in enumerate((top, inner[0], inner[1], inner[2], inner[3], bottom)):
        edge = line[4] * sides
        first = jnp.where(j_of == 0, edge, pltpu.roll(line[3], 1, 1))
        last = jnp.where(j_of == 1, edge, pltpu.roll(line[0], 7, 1))
        for q, tile in enumerate((first, line[0], line[1], line[2], line[3], last)):
            hidden[p, q] = tile.reshape(16, CHANS).astype(BF16)

    load_k2.wait()

    def mix(half):
        convolve(hidden, k2, acc, half)
        before = kept[128 * half : 128 * half + 128].reshape(2, 4, 2, 8, CHANS)
        mixed = (before + joined(acc, 2, 4)).astype(BF16).reshape(8, 16, CHANS)
        for tile in range(8):
            lat[8 * half + tile, zh, y] = mixed[tile]

    zs = [zh] + [lax.rem(zh + step, RING) for step in (1, 2, 3)]
    ys = [y] + [lax.rem(y + step, RING) for step in (1, 2, 3)]
    pending = []
    near, far, near2, far2 = {}, {}, {}, {}

    def pieces(c, u, v, part=None):
        first, last, y_first = PARTS[c]
        if part is not None:
            middle = (first + last) // 2
            first, last = (first, middle) if part == 0 else (middle, last)
        a, b = (zs[v], ys[u]) if y_first else (zs[u], ys[v])
        return lat.at[pl.ds(first, last - first), a, b]

    def straight(c, u):
        return any(move == "D%d%d" % (c, u) for move in ORDER)

    def pass_on(piece, send_sem, recv_sem, device):
        copy = send(piece, piece, send_sem, recv_sem, device)
        pending.append(copy)
        return copy

    def multiply(c, which, taps):
        first, last, y_first = PARTS[c]
        for b in taps:
            part = None
            for tile in range(first, last):
                block = jnp.concatenate(
                    [(lat[tile, :, ys[u]] if y_first else lat[tile, zs[u]]).reshape(64, CHANS) for u in which], axis=0
                )
                term = lax.dot_general(
                    block,
                    w[b, :, tile * CHANS : (tile + 1) * CHANS],
                    (((1,), (1,)), ((), ())),
                    preferred_element_type=F32,
                )
                part = term if part is None else part + term
            for at, u in enumerate(which):
                term = part[at * 64 : (at + 1) * 64].reshape(RING, 16, 3 * OUT_DEV)
                if y_first:
                    y_acc[b, :, ys[u]] += term
                else:
                    y_acc[b, zs[u]] += term

    for move in ORDER:
        what, c, u = move[0], int(move[1]), int(move[2:3] or 0)
        if what == "C":
            mix(c)
            continue
        rings = (to_y, to_z) if PARTS[c][2] else (to_z, to_y)
        opposite = (to_y2, to_z2) if PARTS[c][2] else (to_z2, to_y2)
        if what == "n":
            near[c] = [
                pass_on(pieces(c, 0, 0), near_send.at[c, d], near_recv.at[c, d], rings[0][d]) for d in range(2)
            ]
        elif what == "f":
            for copy in near[c]:
                copy.wait_recv()
            far[c] = [
                pass_on(pieces(c, 3 - 2 * d, 0, d), far_send.at[c, d], far_recv.at[c, d], rings[0][d]) for d in range(2)
            ]
        elif what == "d":
            far[c] = [pass_on(pieces(c, 0, 0), far_send.at[c, 0], far_recv.at[c, 0], opposite[0])]
        elif what == "e":
            for copy in near[c]:
                copy.wait_recv()
        elif what in "ND":
            if u == 2:
                for copy in far[c]:
                    copy.wait_recv()
            near2[c, u] = [
                pass_on(pieces(c, u, 0), near2_send.at[c, u, d], near2_recv.at[c, u, d], rings[1][d]) for d in range(2)
            ]
            if what == "D":
                far2[c, u] = pass_on(pieces(c, u, 0), far2_send.at[c, u], far2_recv.at[c, u], opposite[1])
        elif what == "F":
            for copy in near2[c, u]:
                copy.wait_recv()
            d = (0, 1, 1, 0)[u] if c % 2 == 0 else (1, 1, 0, 0)[u]
            far2[c, u] = pass_on(pieces(c, u, 3 - 2 * d), far2_send.at[c, u], far2_recv.at[c, u], rings[1][d])
        else:
            for copy in w_loads:
                copy.wait()
            w_loads = []
            which = [int(u) for u in move[2:]]
            for u in which:
                if straight(c, u):
                    for copy in near2[c, u]:
                        copy.wait_recv()
                far2[c, u].wait_recv()
            if move != ORDER[-1]:
                multiply(c, which, range(3))

    s = lax.broadcasted_iota(jnp.int32, (1, 16, OUT_DEV), 1) % 2
    edge = jnp.zeros((1, 16, OUT_DEV), F32)

    def moved(b):
        sums = y_acc[b].reshape(PIECES, 16, 3 * OUT_DEV)
        first, second, third = (sums[..., e * OUT_DEV : (e + 1) * OUT_DEV] for e in range(3))
        from_left = jnp.concatenate([edge, pltpu.roll(first, 15, 1)[: PIECES - 1]], axis=0)
        from_right = jnp.concatenate([pltpu.roll(third, 1, 1)[1:], edge], axis=0)
        total = second + jnp.where(s == 1, pltpu.roll(first, 1, 1), from_left)
        total += jnp.where(s == 0, pltpu.roll(third, 15, 1), from_right)
        return total.reshape(PIECES, 2, 8, OUT_DEV)

    def pack(part):
        return jnp.concatenate([part[:8].reshape(64, OUT_DEV), part[8:].reshape(64, OUT_DEV)], axis=1)

    multiply(c, which, (0, 2))
    above, below = moved(0), moved(2)
    u_out[0] = pack(below[:, 0])
    u_out[1] = pack(above[:, 1])
    rows_sent = [
        send(u_out.at[0], u_in.at[1], u_send.at[0], u_recv.at[0], (up, col)),
        send(u_out.at[1], u_in.at[0], u_send.at[1], u_recv.at[1], (down, col)),
    ]
    multiply(c, which, (1,))
    load_mean.wait()
    centre = lat[col].reshape(256, CHANS)
    shortcut = jnp.dot(centre, g_mean[...], preferred_element_type=F32).reshape(PIECES, 2, 8, OUT_DEV)
    same = moved(1) + shortcut
    result0 = same[:, 0] + below[:, 1]
    result1 = same[:, 1] + above[:, 0]

    for copy in rows_sent:
        copy.wait_recv()

    def unpack(part, there):
        part = jnp.where(there, part, 0.0)
        return jnp.concatenate(
            [part[:, :OUT_DEV].reshape(8, 8, OUT_DEV), part[:, OUT_DEV:].reshape(8, 8, OUT_DEV)], axis=0
        )

    out_ref[0] = (result0 + unpack(u_in[0], has_up)).reshape(128, OUT_DEV).astype(BF16)
    out_ref[1] = (result1 + unpack(u_in[1], has_down)).reshape(128, OUT_DEV).astype(BF16)
    for copy in sent + pending + rows_sent:
        copy.wait_send()


def per_device(n_row, n_col, frames_in, norm_gain, first_kernel, second_kernel, latent_kernel):
    g_own, g_halo = spread_tables()
    anywhere = pl.BlockSpec(memory_space=pltpu.HBM)
    dma = pltpu.SemaphoreType.DMA
    out = pl.pallas_call(
        functools.partial(kernel, n_row, n_col),
        out_shape=jax.ShapeDtypeStruct((2, 128, OUT_DEV), BF16),
        in_specs=[anywhere] * 9,
        out_specs=pl.BlockSpec(memory_space=pltpu.VMEM),
        scratch_shapes=[
            pltpu.VMEM((4, 4, 16, CHANS), BF16),
            pltpu.VMEM((1, CHANS), F32),
            pltpu.VMEM((3, 3, 3, CHANS, CHANS), BF16),
            pltpu.VMEM((3, 3, 3, CHANS, CHANS), BF16),
            pltpu.VMEM((3, 3 * OUT_DEV, LATENT), BF16),
            pltpu.VMEM((81 * 16, 256), BF16),
            pltpu.VMEM((65 * 16, 384), BF16),
            pltpu.VMEM((128, 256), BF16),
            pltpu.VMEM((CHANS, OUT_DEV), BF16),
            pltpu.VMEM((2, 4, 16, CHANS), BF16),
            pltpu.VMEM((20, 16, CHANS), BF16),
            pltpu.VMEM((24, 16, CHANS), BF16),
            pltpu.VMEM((9, 9, 16, CHANS), BF16),
            pltpu.VMEM((65 * 16, CHANS), F32),
            pltpu.VMEM((6, 6, 16, CHANS), BF16),
            pltpu.VMEM((3, 5, 5, 16, CHANS), F32),
            pltpu.VMEM((PIECES, RING, RING, 16, CHANS), BF16),
            pltpu.VMEM((3, RING, RING, 16, 3 * OUT_DEV), F32),
            pltpu.VMEM((2, 64, 2 * OUT_DEV), F32),
            pltpu.VMEM((2, 64, 2 * OUT_DEV), F32),
            pltpu.VMEM((256, CHANS), F32),
            dma((8,)),
            dma((3,)),
            dma((8,)),
            dma((8,)),
            dma((CHUNKS, 2)),
            dma((CHUNKS, 2)),
            dma((CHUNKS, 2)),
            dma((CHUNKS, 2)),
            dma((CHUNKS, RING, 2)),
            dma((CHUNKS, RING, 2)),
            dma((CHUNKS, RING)),
            dma((CHUNKS, RING)),
            dma((2,)),
            dma((2,)),
        ],
        compiler_params=pltpu.CompilerParams(
            collective_id=0, has_side_effects=True, vmem_limit_bytes=60 << 20
        ),
        cost_estimate=pl.CostEstimate(flops=4 << 30, bytes_accessed=14 << 20, transcendentals=1 << 18),
    )(
        frames_in.reshape(4, 4, 16, CHANS),
        norm_gain.reshape(1, CHANS),
        first_kernel,
        second_kernel,
        latent_kernel.transpose(0, 1, 3, 2).reshape(3, 3 * OUT_DEV, LATENT),
        g_own,
        g_halo,
        strip_table(),
        mean_table(),
    )
    out = out.reshape(2, PIECES, FRAMES, 2, OUT_DEV)
    return out.transpose(2, 0, 1, 3, 4).reshape(FRAMES, 2, 2 * PIECES, OUT_DEV)


def solution(mesh):
    return jax.shard_map(
        functools.partial(per_device, mesh.shape["row"], mesh.shape["col"]),
        mesh=mesh,
        in_specs=(P(None, "row", "col", None), P(), P(), P(), P(None, None, None, "col")),
        out_specs=P(None, "row", None, "col"),
        check_vma=False,
    )
```

```python
import functools

import jax
import jax.numpy as jnp
import numpy as np
from jax import lax
from jax.experimental import pallas as pl
from jax.experimental.pallas import tpu as pltpu
from jax.sharding import PartitionSpec as P

MESH = pl.DeviceIdType.MESH
F32 = jnp.float32
BF16 = jnp.bfloat16
FRAMES, SIDE, CHANS = 4, 8, 256
OUT_CH, LATENT = 1024, 4096
RING = 4
PIECES = RING * RING
OUT_DEV = OUT_CH // PIECES
PARTS = ((0, 6, False), (6, 12, False), (12, 16, True))
CHUNKS = len(PARTS)
ORDER = (
    ("C0", "C1", "n0", "n2", "d2", "N00", "n1", "N10", "e2", "f0", "N01", "N03", "f1", "N11", "N13", "N20", "N21", "N23", "N22")
    + ("F00", "F10", "D02", "D12", "F01", "F03", "F11", "F13", "F20", "F21", "F23", "F22", "W00132", "W10132", "W20132")
)


def one_hot(index, width):
    out = np.zeros((len(index), width), np.float32)
    for at, source in enumerate(index):
        if source >= 0:
            out[at, source] = 1
    return out.astype(BF16)


OWN_TILES = [(p, q) for p in range(1, 5) for q in range(1, 5)]
CORNER_TILES = [(p, q) for p in (0, 5, 6, 7, 8) for q in (0, 5, 6, 7, 8)]
SIDE_TILES = [(p, q) for p in range(9) for q in range(9) if (p, q) not in OWN_TILES + CORNER_TILES]


def line_of(tile, half):
    if tile < 6:
        return 4 * half + tile - 1
    return tile - 6 + (7 if half else -2)


def spread_tables():
    own, halo = [], []
    for p, q in OWN_TILES + SIDE_TILES + CORNER_TILES:
        for i in range(2):
            for f in range(FRAMES):
                for j in range(2):
                    r, c = line_of(p, i), line_of(q, j)
                    inside_r, inside_c = 0 <= r < SIDE, 0 <= c < SIDE
                    a, b = -1, -1
                    side = 0 if c < 0 else 1
                    cc = c + 2 if c < 0 else c - SIDE
                    rr = r + 2 if r < 0 else r - SIDE
                    if inside_r and inside_c:
                        a = f * 64 + r * 8 + c
                    elif inside_c:
                        b = ((0 if r < 0 else 4) + f) * 16 + rr * 8 + c
                    elif inside_r:
                        b = (8 + 4 * side + r // 2) * 16 + f * 4 + (r % 2) * 2 + cc
                    else:
                        b = (16 + (0 if r < 0 else 2) + side) * 16 + f * 4 + rr * 2 + cc
                    own.append(a)
                    halo.append(b)
    return one_hot(own, 256), one_hot(halo[256:], 384)


def strip_table():
    index = []
    for side in range(2):
        for rp in range(4):
            for f in range(FRAMES):
                for rr in range(2):
                    for cc in range(2):
                        index.append(f * 64 + (2 * rp + rr) * 8 + 6 * side + cc)
    return one_hot(index, 256)


def mean_table():
    group = LATENT // OUT_CH
    out = np.zeros((CHANS, CHANS // group), np.float32)
    out[np.arange(CHANS), np.arange(CHANS) // group] = 1 / group
    return out.astype(BF16)


def convolve_own(cells, w, acc):
    acc[:, 4] = jnp.zeros((3, 5, 16, CHANS), F32)
    acc[:, 0:4, 4] = jnp.zeros((3, 4, 16, CHANS), F32)
    order = [(1, 1)] + [(b, e) for b in range(3) for e in range(3) if (b, e) != (1, 1)]
    for a in range(3):
        for b, e in order:
            p0, p1, q0, q1 = max(0, 1 - b), min(4, 5 - b), max(0, 1 - e), min(4, 5 - e)
            shape = (p1 - p0, q1 - q0, 16, CHANS)
            lhs = cells[p0 + b : p1 + b, q0 + e : q1 + e].reshape(-1, CHANS)
            part = jnp.dot(lhs, w[a, b, e], preferred_element_type=F32).reshape(shape)
            if (b, e) == (1, 1):
                acc[a, 0:4, 0:4] = part
            else:
                acc[a, p0:p1, q0:q1] += part


def convolve_rest(cells, w, acc, sources):
    for a in range(3):
        for b in range(3):
            for e in range(3):
                reads = {
                    (p, q): (p + b if p < 4 else 6 + b, q + e if q < 4 else 6 + e) for p in range(5) for q in range(5)
                }
                tiles = [tile for tile in reads if reads[tile] in sources]
                lhs = jnp.concatenate([cells[reads[tile]] for tile in tiles], axis=0)
                part = jnp.dot(lhs, w[a, b, e], preferred_element_type=F32)
                for at, (p, q) in enumerate(tiles):
                    acc[a, p, q] += part[at * 16 : (at + 1) * 16]


def convolve(src, w, acc, half):
    for a in range(3):
        total = None
        for b in range(3):
            for e in range(3):
                lhs = src[2 * half + b : 2 * half + b + 2, e : e + 4].reshape(128, CHANS)
                part = jnp.dot(lhs, w[a, b, e], preferred_element_type=F32)
                total = part if total is None else total + part
        acc[a, 0:2, 0:4] = total.reshape(2, 4, 16, CHANS)


def joined(acc, m, n):
    early, same, late = (acc[a, 0:m, 0:n].reshape(m * n * 2, 8, CHANS) for a in range(3))
    f = lax.broadcasted_iota(jnp.int32, (1, 8, CHANS), 1) // 2
    total = same + jnp.where(f > 0, pltpu.roll(early, 2, 1), 0.0)
    total += jnp.where(f < FRAMES - 1, pltpu.roll(late, 6, 1), 0.0)
    return total.reshape(m, n, 2, 8, CHANS)


def kernel(
    n_row, n_col,
    x_hbm, gain_hbm, k1_hbm, k2_hbm, w_hbm, g_own_hbm, g_halo_hbm, g_strip_hbm, g_mean_hbm,
    out_ref,
    x, gain, k1, k2, w, g_own, g_halo, g_strip, g_mean,
    strips, halo, normed, cells, others, hidden, acc, lat, y_acc, u_out, u_in, kept,
    load_sem, w_sem, halo_send, halo_recv,
    near_send, near_recv, far_send, far_recv, near2_send, near2_recv, far2_send, far2_recv,
    u_send, u_recv,
):
    row, col = lax.axis_index("row"), lax.axis_index("col")
    zh, y = col // RING, col % RING
    up, down = lax.rem(row + n_row - 1, n_row), lax.rem(row + 1, n_row)
    left, right = lax.rem(col + n_col - 1, n_col), lax.rem(col + 1, n_col)
    z_next, z_prev = lax.rem(zh + 1, RING), lax.rem(zh + RING - 1, RING)
    y_next, y_prev = lax.rem(y + 1, RING), lax.rem(y + RING - 1, RING)
    to_z = ((row, z_next * RING + y), (row, z_prev * RING + y))
    to_y = ((row, zh * RING + y_next), (row, zh * RING + y_prev))

    to_z2 = (row, lax.rem(zh + 2, RING) * RING + y)
    to_y2 = (row, zh * RING + lax.rem(y + 2, RING))

    barrier = pltpu.get_barrier_semaphore()
    around = (
        (up, col), (down, col), (row, left), (row, right),
        (up, left), (up, right), (down, left), (down, right),
    ) + to_z + to_y + (to_z2, to_y2)
    for target in around:
        pl.semaphore_signal(barrier, inc=1, device_id=target, device_id_type=MESH)

    loads = []
    for at, (source, target) in enumerate((
        (x_hbm, x), (g_strip_hbm, g_strip), (gain_hbm, gain), (g_own_hbm, g_own), (k1_hbm, k1),
        (g_halo_hbm, g_halo), (k2_hbm, k2), (g_mean_hbm, g_mean),
    )):
        copy = pltpu.make_async_copy(source, target, load_sem.at[at])
        copy.start()
        loads.append(copy)
    w_loads = []
    for b in range(3):
        copy = pltpu.make_async_copy(w_hbm.at[b], w.at[b], w_sem.at[b])
        copy.start()
        w_loads.append(copy)
    load_x, load_strip, load_gain, load_own, load_k1, load_halo, load_k2, load_mean = loads

    def send(source, target, send_sem, recv_sem, device):
        copy = pltpu.make_async_remote_copy(
            src_ref=source, dst_ref=target, send_sem=send_sem, recv_sem=recv_sem, device_id=device, device_id_type=MESH
        )
        copy.start()
        return copy

    load_x.wait()
    load_strip.wait()
    own = x[...].reshape(256, CHANS)
    strips[...] = jnp.dot(g_strip[...], own, preferred_element_type=F32).astype(BF16).reshape(2, 4, 16, CHANS)
    pl.semaphore_wait(barrier, len(around))
    sent = [
        send(strips.at[0, 3], halo.at[17], halo_send.at[4], halo_recv.at[4], (down, left)),
        send(strips.at[1, 3], halo.at[16], halo_send.at[5], halo_recv.at[5], (down, right)),
        send(strips.at[0, 0], halo.at[19], halo_send.at[6], halo_recv.at[6], (up, left)),
        send(strips.at[1, 0], halo.at[18], halo_send.at[7], halo_recv.at[7], (up, right)),
        send(x.at[:, 0], halo.at[pl.ds(4, 4)], halo_send.at[0], halo_recv.at[0], (up, col)),
        send(x.at[:, 3], halo.at[pl.ds(0, 4)], halo_send.at[1], halo_recv.at[1], (down, col)),
        send(strips.at[0], halo.at[pl.ds(12, 4)], halo_send.at[2], halo_recv.at[2], (row, left)),
        send(strips.at[1], halo.at[pl.ds(8, 4)], halo_send.at[3], halo_recv.at[3], (row, right)),
    ]

    load_gain.wait()

    def norm(raw):
        values = raw.astype(F32)
        scale = lax.rsqrt(jnp.mean(values * values, axis=-1, keepdims=True) + 1e-06)
        return values * scale * gain[...]

    own_normed = norm(own).astype(BF16)
    normed[20:24] = jnp.zeros((4, 16, CHANS), BF16)
    y_acc[...] = jnp.zeros(y_acc.shape, F32)
    load_own.wait()
    middle = jnp.dot(g_own[0:256], own_normed, preferred_element_type=F32)
    cells[1:5, 1:5] = middle.astype(BF16).reshape(4, 4, 16, CHANS)
    load_k1.wait()
    convolve_own(cells, k1, acc)
    others[...] = jnp.dot(g_own[256:], own_normed, preferred_element_type=F32)
    kept[...] = jnp.dot(g_own[0:256], own, preferred_element_type=F32)
    load_halo.wait()

    has_up, has_down = row > 0, row < n_row - 1
    has_left, has_right = col > 0, col < n_col - 1

    def norm_halo(parts):
        for start, count, there in parts:
            values = norm(halo[start : start + count].reshape(count * 16, CHANS))
            values = values * jnp.where(there, 1.0, 0.0).astype(F32)
            normed[start : start + count] = values.astype(BF16).reshape(count, 16, CHANS)

    sides_at = 16 * len(SIDE_TILES)
    for copy in sent[4:]:
        copy.wait_recv()
    norm_halo(((0, 4, has_up), (4, 4, has_down), (8, 4, has_left), (12, 4, has_right)))
    spread = others[...] + jnp.dot(
        g_halo[:, 0:256], normed[0:16].reshape(256, CHANS), preferred_element_type=F32
    )
    for at, (p, q) in enumerate(SIDE_TILES):
        cells[p, q] = spread[at * 16 : (at + 1) * 16].astype(BF16)
    others[sides_at:] = spread[sides_at:]
    convolve_rest(cells, k1, acc, SIDE_TILES)

    for copy in sent[:4]:
        copy.wait_recv()
    norm_halo((
        (16, 1, has_up & has_left), (17, 1, has_up & has_right),
        (18, 1, has_down & has_left), (19, 1, has_down & has_right),
    ))
    spread = others[sides_at:] + jnp.dot(
        g_halo[sides_at:, 256:384], normed[16:24].reshape(128, CHANS), preferred_element_type=F32
    )
    for at, (p, q) in enumerate(CORNER_TILES):
        cells[p, q] = spread[at * 16 : (at + 1) * 16].astype(BF16)
    convolve_rest(cells, k1, acc, CORNER_TILES)

    value = joined(acc, 5, 5)
    value = value / (1.0 + jnp.exp(-value))
    def flag(there):
        return jnp.where(there, 1.0, 0.0).astype(F32)

    j_of = lax.broadcasted_iota(jnp.int32, (1, 8, CHANS), 1) % 2
    sides = jnp.where(j_of == 0, flag(has_left), flag(has_right))
    inner, below = value[0:4], value[4]
    top = jnp.stack([below[:, 0] * flag(has_up), inner[3][:, 0]], axis=1)
    bottom = jnp.stack([inner[0][:, 1], below[:, 1] * flag(has_down)], axis=1)
    for p, line in enumerate((top, inner[0], inner[1], inner[2], inner[3], bottom)):
        edge = line[4] * sides
        first = jnp.where(j_of == 0, edge, pltpu.roll(line[3], 1, 1))
        last = jnp.where(j_of == 1, edge, pltpu.roll(line[0], 7, 1))
        for q, tile in enumerate((first, line[0], line[1], line[2], line[3], last)):
            hidden[p, q] = tile.reshape(16, CHANS).astype(BF16)

    load_k2.wait()

    def mix(half):
        convolve(hidden, k2, acc, half)
        before = kept[128 * half : 128 * half + 128].reshape(2, 4, 2, 8, CHANS)
        mixed = (before + joined(acc, 2, 4)).astype(BF16).reshape(8, 16, CHANS)
        for tile in range(8):
            lat[8 * half + tile, zh, y] = mixed[tile]

    zs = [zh] + [lax.rem(zh + step, RING) for step in (1, 2, 3)]
    ys = [y] + [lax.rem(y + step, RING) for step in (1, 2, 3)]
    pending = []
    near, far, near2, far2 = {}, {}, {}, {}

    def pieces(c, u, v, part=None):
        first, last, y_first = PARTS[c]
        if part is not None:
            middle = (first + last) // 2
            first, last = (first, middle) if part == 0 else (middle, last)
        a, b = (zs[v], ys[u]) if y_first else (zs[u], ys[v])
        return lat.at[pl.ds(first, last - first), a, b]

    def straight(c, u):
        return any(move == "D%d%d" % (c, u) for move in ORDER)

    def pass_on(piece, send_sem, recv_sem, device):
        copy = send(piece, piece, send_sem, recv_sem, device)
        pending.append(copy)
        return copy

    def multiply(c, which, taps):
        first, last, y_first = PARTS[c]
        for b in taps:
            part = None
            for tile in range(first, last):
                block = jnp.concatenate(
                    [(lat[tile, :, ys[u]] if y_first else lat[tile, zs[u]]).reshape(64, CHANS) for u in which], axis=0
                )
                term = lax.dot_general(
                    block,
                    w[b, :, tile * CHANS : (tile + 1) * CHANS],
                    (((1,), (1,)), ((), ())),
                    preferred_element_type=F32,
                )
                part = term if part is None else part + term
            for at, u in enumerate(which):
                term = part[at * 64 : (at + 1) * 64].reshape(RING, 16, 3 * OUT_DEV)
                if y_first:
                    y_acc[b, :, ys[u]] += term
                else:
                    y_acc[b, zs[u]] += term

    for move in ORDER:
        what, c, u = move[0], int(move[1]), int(move[2:3] or 0)
        if what == "C":
            mix(c)
            continue
        rings = (to_y, to_z) if PARTS[c][2] else (to_z, to_y)
        opposite = (to_y2, to_z2) if PARTS[c][2] else (to_z2, to_y2)
        if what == "n":
            near[c] = [
                pass_on(pieces(c, 0, 0), near_send.at[c, d], near_recv.at[c, d], rings[0][d]) for d in range(2)
            ]
        elif what == "f":
            for copy in near[c]:
                copy.wait_recv()
            far[c] = [
                pass_on(pieces(c, 3 - 2 * d, 0, d), far_send.at[c, d], far_recv.at[c, d], rings[0][d]) for d in range(2)
            ]
        elif what == "d":
            far[c] = [pass_on(pieces(c, 0, 0), far_send.at[c, 0], far_recv.at[c, 0], opposite[0])]
        elif what == "e":
            for copy in near[c]:
                copy.wait_recv()
        elif what in "ND":
            if u == 2:
                for copy in far[c]:
                    copy.wait_recv()
            near2[c, u] = [
                pass_on(pieces(c, u, 0), near2_send.at[c, u, d], near2_recv.at[c, u, d], rings[1][d]) for d in range(2)
            ]
            if what == "D":
                far2[c, u] = pass_on(pieces(c, u, 0), far2_send.at[c, u], far2_recv.at[c, u], opposite[1])
        elif what == "F":
            for copy in near2[c, u]:
                copy.wait_recv()
            d = (0, 1, 1, 0)[u] if c % 2 == 0 else (1, 1, 0, 0)[u]
            far2[c, u] = pass_on(pieces(c, u, 3 - 2 * d), far2_send.at[c, u], far2_recv.at[c, u], rings[1][d])
        else:
            for copy in w_loads:
                copy.wait()
            w_loads = []
            which = [int(u) for u in move[2:]]
            for u in which:
                if straight(c, u):
                    for copy in near2[c, u]:
                        copy.wait_recv()
                far2[c, u].wait_recv()
            multiply(c, which, (0, 2))

    s = lax.broadcasted_iota(jnp.int32, (1, 16, OUT_DEV), 1) % 2
    edge = jnp.zeros((1, 16, OUT_DEV), F32)

    def moved(b):
        sums = y_acc[b].reshape(PIECES, 16, 3 * OUT_DEV)
        first, second, third = (sums[..., e * OUT_DEV : (e + 1) * OUT_DEV] for e in range(3))
        from_left = jnp.concatenate([edge, pltpu.roll(first, 15, 1)[: PIECES - 1]], axis=0)
        from_right = jnp.concatenate([pltpu.roll(third, 1, 1)[1:], edge], axis=0)
        total = second + jnp.where(s == 1, pltpu.roll(first, 1, 1), from_left)
        total += jnp.where(s == 0, pltpu.roll(third, 15, 1), from_right)
        return total.reshape(PIECES, 2, 8, OUT_DEV)

    def pack(part):
        return jnp.concatenate([part[:8].reshape(64, OUT_DEV), part[8:].reshape(64, OUT_DEV)], axis=1)

    above, below = moved(0), moved(2)
    u_out[0] = pack(below[:, 0])
    u_out[1] = pack(above[:, 1])
    rows_sent = [
        send(u_out.at[0], u_in.at[1], u_send.at[0], u_recv.at[0], (up, col)),
        send(u_out.at[1], u_in.at[0], u_send.at[1], u_recv.at[1], (down, col)),
    ]
    for c in range(CHUNKS):
        multiply(c, range(RING), (1,))
    load_mean.wait()
    centre = lat[col].reshape(256, CHANS)
    shortcut = jnp.dot(centre, g_mean[...], preferred_element_type=F32).reshape(PIECES, 2, 8, OUT_DEV)
    same = moved(1) + shortcut
    result0 = same[:, 0] + below[:, 1]
    result1 = same[:, 1] + above[:, 0]

    for copy in rows_sent:
        copy.wait_recv()

    def unpack(part, there):
        part = jnp.where(there, part, 0.0)
        return jnp.concatenate(
            [part[:, :OUT_DEV].reshape(8, 8, OUT_DEV), part[:, OUT_DEV:].reshape(8, 8, OUT_DEV)], axis=0
        )

    out_ref[0] = (result0 + unpack(u_in[0], has_up)).reshape(128, OUT_DEV).astype(BF16)
    out_ref[1] = (result1 + unpack(u_in[1], has_down)).reshape(128, OUT_DEV).astype(BF16)
    for copy in sent + pending + rows_sent:
        copy.wait_send()


def per_device(n_row, n_col, frames_in, norm_gain, first_kernel, second_kernel, latent_kernel):
    g_own, g_halo = spread_tables()
    anywhere = pl.BlockSpec(memory_space=pltpu.HBM)
    dma = pltpu.SemaphoreType.DMA
    out = pl.pallas_call(
        functools.partial(kernel, n_row, n_col),
        out_shape=jax.ShapeDtypeStruct((2, 128, OUT_DEV), BF16),
        in_specs=[anywhere] * 9,
        out_specs=pl.BlockSpec(memory_space=pltpu.VMEM),
        scratch_shapes=[
            pltpu.VMEM((4, 4, 16, CHANS), BF16),
            pltpu.VMEM((1, CHANS), F32),
            pltpu.VMEM((3, 3, 3, CHANS, CHANS), BF16),
            pltpu.VMEM((3, 3, 3, CHANS, CHANS), BF16),
            pltpu.VMEM((3, 3 * OUT_DEV, LATENT), BF16),
            pltpu.VMEM((81 * 16, 256), BF16),
            pltpu.VMEM((65 * 16, 384), BF16),
            pltpu.VMEM((128, 256), BF16),
            pltpu.VMEM((CHANS, OUT_DEV), BF16),
            pltpu.VMEM((2, 4, 16, CHANS), BF16),
            pltpu.VMEM((20, 16, CHANS), BF16),
            pltpu.VMEM((24, 16, CHANS), BF16),
            pltpu.VMEM((9, 9, 16, CHANS), BF16),
            pltpu.VMEM((65 * 16, CHANS), F32),
            pltpu.VMEM((6, 6, 16, CHANS), BF16),
            pltpu.VMEM((3, 5, 5, 16, CHANS), F32),
            pltpu.VMEM((PIECES, RING, RING, 16, CHANS), BF16),
            pltpu.VMEM((3, RING, RING, 16, 3 * OUT_DEV), F32),
            pltpu.VMEM((2, 64, 2 * OUT_DEV), F32),
            pltpu.VMEM((2, 64, 2 * OUT_DEV), F32),
            pltpu.VMEM((256, CHANS), F32),
            dma((8,)),
            dma((3,)),
            dma((8,)),
            dma((8,)),
            dma((CHUNKS, 2)),
            dma((CHUNKS, 2)),
            dma((CHUNKS, 2)),
            dma((CHUNKS, 2)),
            dma((CHUNKS, RING, 2)),
            dma((CHUNKS, RING, 2)),
            dma((CHUNKS, RING)),
            dma((CHUNKS, RING)),
            dma((2,)),
            dma((2,)),
        ],
        compiler_params=pltpu.CompilerParams(
            collective_id=0, has_side_effects=True, vmem_limit_bytes=60 << 20
        ),
        cost_estimate=pl.CostEstimate(flops=4 << 30, bytes_accessed=14 << 20, transcendentals=1 << 18),
    )(
        frames_in.reshape(4, 4, 16, CHANS),
        norm_gain.reshape(1, CHANS),
        first_kernel,
        second_kernel,
        latent_kernel.transpose(0, 1, 3, 2).reshape(3, 3 * OUT_DEV, LATENT),
        g_own,
        g_halo,
        strip_table(),
        mean_table(),
    )
    out = out.reshape(2, PIECES, FRAMES, 2, OUT_DEV)
    return out.transpose(2, 0, 1, 3, 4).reshape(FRAMES, 2, 2 * PIECES, OUT_DEV)


def solution(mesh):
    return jax.shard_map(
        functools.partial(per_device, mesh.shape["row"], mesh.shape["col"]),
        mesh=mesh,
        in_specs=(P(None, "row", "col", None), P(), P(), P(), P(None, None, None, "col")),
        out_specs=P(None, "row", None, "col"),
        check_vma=False,
    )
```

```python
import functools

import jax
import jax.numpy as jnp
import numpy as np
from jax import lax
from jax.experimental import pallas as pl
from jax.experimental.pallas import tpu as pltpu
from jax.sharding import PartitionSpec as P

MESH = pl.DeviceIdType.MESH
F32 = jnp.float32
BF16 = jnp.bfloat16
FRAMES, SIDE, CHANS = 4, 8, 256
OUT_CH, LATENT = 1024, 4096
RING = 4
PIECES = RING * RING
OUT_DEV = OUT_CH // PIECES
PARTS = ((0, 6, False), (6, 12, False), (12, 16, True))
CHUNKS = len(PARTS)
ORDER = (
    ("C0", "n0", "N00", "C1", "n2", "d2", "n1", "N10", "e2", "f0", "N01", "N03", "f1", "N11", "N13", "N20", "N21", "N23", "N22")
    + ("F00", "F10", "D02", "D12", "F01", "F03", "F11", "F13", "F20", "F21", "F23", "F22", "W00132", "W10132", "W20132")
)


def one_hot(index, width):
    out = np.zeros((len(index), width), np.float32)
    for at, source in enumerate(index):
        if source >= 0:
            out[at, source] = 1
    return out.astype(BF16)


OWN_TILES = [(p, q) for p in range(1, 5) for q in range(1, 5)]
CORNER_TILES = [(p, q) for p in (0, 5, 6, 7, 8) for q in (0, 5, 6, 7, 8)]
SIDE_TILES = [(p, q) for p in range(9) for q in range(9) if (p, q) not in OWN_TILES + CORNER_TILES]


def line_of(tile, half):
    if tile < 6:
        return 4 * half + tile - 1
    return tile - 6 + (7 if half else -2)


def spread_tables():
    own, halo = [], []
    for p, q in OWN_TILES + SIDE_TILES + CORNER_TILES:
        for i in range(2):
            for f in range(FRAMES):
                for j in range(2):
                    r, c = line_of(p, i), line_of(q, j)
                    inside_r, inside_c = 0 <= r < SIDE, 0 <= c < SIDE
                    a, b = -1, -1
                    side = 0 if c < 0 else 1
                    cc = c + 2 if c < 0 else c - SIDE
                    rr = r + 2 if r < 0 else r - SIDE
                    if inside_r and inside_c:
                        a = f * 64 + r * 8 + c
                    elif inside_c:
                        b = ((0 if r < 0 else 4) + f) * 16 + rr * 8 + c
                    elif inside_r:
                        b = (8 + 4 * side + r // 2) * 16 + f * 4 + (r % 2) * 2 + cc
                    else:
                        b = (16 + (0 if r < 0 else 2) + side) * 16 + f * 4 + rr * 2 + cc
                    own.append(a)
                    halo.append(b)
    return one_hot(own, 256), one_hot(halo[256:], 384)


def strip_table():
    index = []
    for side in range(2):
        for rp in range(4):
            for f in range(FRAMES):
                for rr in range(2):
                    for cc in range(2):
                        index.append(f * 64 + (2 * rp + rr) * 8 + 6 * side + cc)
    return one_hot(index, 256)


def mean_table():
    group = LATENT // OUT_CH
    out = np.zeros((CHANS, CHANS // group), np.float32)
    out[np.arange(CHANS), np.arange(CHANS) // group] = 1 / group
    return out.astype(BF16)


def convolve_own(cells, w, acc):
    acc[:, 4] = jnp.zeros((3, 5, 16, CHANS), F32)
    acc[:, 0:4, 4] = jnp.zeros((3, 4, 16, CHANS), F32)
    order = [(1, 1)] + [(b, e) for b in range(3) for e in range(3) if (b, e) != (1, 1)]
    for a in range(3):
        for b, e in order:
            p0, p1, q0, q1 = max(0, 1 - b), min(4, 5 - b), max(0, 1 - e), min(4, 5 - e)
            shape = (p1 - p0, q1 - q0, 16, CHANS)
            lhs = cells[p0 + b : p1 + b, q0 + e : q1 + e].reshape(-1, CHANS)
            part = jnp.dot(lhs, w[a, b, e], preferred_element_type=F32).reshape(shape)
            if (b, e) == (1, 1):
                acc[a, 0:4, 0:4] = part
            else:
                acc[a, p0:p1, q0:q1] += part


def convolve_rest(cells, w, acc, sources):
    for a in range(3):
        for b in range(3):
            for e in range(3):
                reads = {
                    (p, q): (p + b if p < 4 else 6 + b, q + e if q < 4 else 6 + e) for p in range(5) for q in range(5)
                }
                tiles = [tile for tile in reads if reads[tile] in sources]
                lhs = jnp.concatenate([cells[reads[tile]] for tile in tiles], axis=0)
                part = jnp.dot(lhs, w[a, b, e], preferred_element_type=F32)
                for at, (p, q) in enumerate(tiles):
                    acc[a, p, q] += part[at * 16 : (at + 1) * 16]


def convolve(src, w, acc, half):
    for a in range(3):
        total = None
        for b in range(3):
            for e in range(3):
                lhs = src[2 * half + b : 2 * half + b + 2, e : e + 4].reshape(128, CHANS)
                part = jnp.dot(lhs, w[a, b, e], preferred_element_type=F32)
                total = part if total is None else total + part
        acc[a, 0:2, 0:4] = total.reshape(2, 4, 16, CHANS)


def joined(acc, m, n):
    early, same, late = (acc[a, 0:m, 0:n].reshape(m * n * 2, 8, CHANS) for a in range(3))
    f = lax.broadcasted_iota(jnp.int32, (1, 8, CHANS), 1) // 2
    total = same + jnp.where(f > 0, pltpu.roll(early, 2, 1), 0.0)
    total += jnp.where(f < FRAMES - 1, pltpu.roll(late, 6, 1), 0.0)
    return total.reshape(m, n, 2, 8, CHANS)


def kernel(
    n_row, n_col,
    x_hbm, gain_hbm, k1_hbm, k2_hbm, w_hbm, g_own_hbm, g_halo_hbm, g_strip_hbm, g_mean_hbm,
    out_ref,
    x, gain, k1, k2, w, g_own, g_halo, g_strip, g_mean,
    strips, halo, normed, cells, others, hidden, acc, lat, y_acc, u_out, u_in, kept,
    load_sem, w_sem, halo_send, halo_recv,
    near_send, near_recv, far_send, far_recv, near2_send, near2_recv, far2_send, far2_recv,
    u_send, u_recv,
):
    row, col = lax.axis_index("row"), lax.axis_index("col")
    zh, y = col // RING, col % RING
    up, down = lax.rem(row + n_row - 1, n_row), lax.rem(row + 1, n_row)
    left, right = lax.rem(col + n_col - 1, n_col), lax.rem(col + 1, n_col)
    z_next, z_prev = lax.rem(zh + 1, RING), lax.rem(zh + RING - 1, RING)
    y_next, y_prev = lax.rem(y + 1, RING), lax.rem(y + RING - 1, RING)
    to_z = ((row, z_next * RING + y), (row, z_prev * RING + y))
    to_y = ((row, zh * RING + y_next), (row, zh * RING + y_prev))

    to_z2 = (row, lax.rem(zh + 2, RING) * RING + y)
    to_y2 = (row, zh * RING + lax.rem(y + 2, RING))

    barrier = pltpu.get_barrier_semaphore()
    around = (
        (up, left), (up, right), (down, left), (down, right),
        (up, col), (down, col), (row, left), (row, right),
    ) + to_z + to_y + (to_z2, to_y2)
    for target in around:
        pl.semaphore_signal(barrier, inc=1, device_id=target, device_id_type=MESH)

    loads = []
    for at, (source, target) in enumerate((
        (x_hbm, x), (g_strip_hbm, g_strip), (gain_hbm, gain), (g_own_hbm, g_own), (k1_hbm, k1),
        (g_halo_hbm, g_halo), (k2_hbm, k2), (g_mean_hbm, g_mean),
    )):
        copy = pltpu.make_async_copy(source, target, load_sem.at[at])
        copy.start()
        loads.append(copy)
    w_loads = []
    for b in range(3):
        copy = pltpu.make_async_copy(w_hbm.at[b], w.at[b], w_sem.at[b])
        copy.start()
        w_loads.append(copy)
    load_x, load_strip, load_gain, load_own, load_k1, load_halo, load_k2, load_mean = loads

    def send(source, target, send_sem, recv_sem, device):
        copy = pltpu.make_async_remote_copy(
            src_ref=source, dst_ref=target, send_sem=send_sem, recv_sem=recv_sem, device_id=device, device_id_type=MESH
        )
        copy.start()
        return copy

    load_x.wait()
    load_strip.wait()
    own = x[...].reshape(256, CHANS)
    strips[...] = jnp.dot(g_strip[...], own, preferred_element_type=F32).astype(BF16).reshape(2, 4, 16, CHANS)
    pl.semaphore_wait(barrier, len(around))
    sent = [
        send(strips.at[0, 3], halo.at[17], halo_send.at[4], halo_recv.at[4], (down, left)),
        send(strips.at[1, 3], halo.at[16], halo_send.at[5], halo_recv.at[5], (down, right)),
        send(strips.at[0, 0], halo.at[19], halo_send.at[6], halo_recv.at[6], (up, left)),
        send(strips.at[1, 0], halo.at[18], halo_send.at[7], halo_recv.at[7], (up, right)),
        send(x.at[:, 0], halo.at[pl.ds(4, 4)], halo_send.at[0], halo_recv.at[0], (up, col)),
        send(x.at[:, 3], halo.at[pl.ds(0, 4)], halo_send.at[1], halo_recv.at[1], (down, col)),
        send(strips.at[0], halo.at[pl.ds(12, 4)], halo_send.at[2], halo_recv.at[2], (row, left)),
        send(strips.at[1], halo.at[pl.ds(8, 4)], halo_send.at[3], halo_recv.at[3], (row, right)),
    ]

    load_gain.wait()

    def norm(raw):
        values = raw.astype(F32)
        scale = lax.rsqrt(jnp.mean(values * values, axis=-1, keepdims=True) + 1e-06)
        return values * scale * gain[...]

    own_normed = norm(own).astype(BF16)
    normed[20:24] = jnp.zeros((4, 16, CHANS), BF16)
    y_acc[...] = jnp.zeros(y_acc.shape, F32)
    load_own.wait()
    middle = jnp.dot(g_own[0:256], own_normed, preferred_element_type=F32)
    cells[1:5, 1:5] = middle.astype(BF16).reshape(4, 4, 16, CHANS)
    load_k1.wait()
    convolve_own(cells, k1, acc)
    others[...] = jnp.dot(g_own[256:], own_normed, preferred_element_type=F32)
    kept[...] = jnp.dot(g_own[0:256], own, preferred_element_type=F32)
    load_halo.wait()

    has_up, has_down = row > 0, row < n_row - 1
    has_left, has_right = col > 0, col < n_col - 1

    def norm_halo(parts):
        for start, count, there in parts:
            values = norm(halo[start : start + count].reshape(count * 16, CHANS))
            values = values * jnp.where(there, 1.0, 0.0).astype(F32)
            normed[start : start + count] = values.astype(BF16).reshape(count, 16, CHANS)

    sides_at = 16 * len(SIDE_TILES)
    for copy in sent[4:]:
        copy.wait_recv()
    norm_halo(((0, 4, has_up), (4, 4, has_down), (8, 4, has_left), (12, 4, has_right)))
    spread = others[...] + jnp.dot(
        g_halo[:, 0:256], normed[0:16].reshape(256, CHANS), preferred_element_type=F32
    )
    for at, (p, q) in enumerate(SIDE_TILES):
        cells[p, q] = spread[at * 16 : (at + 1) * 16].astype(BF16)
    others[sides_at:] = spread[sides_at:]
    convolve_rest(cells, k1, acc, SIDE_TILES)

    for copy in sent[:4]:
        copy.wait_recv()
    norm_halo((
        (16, 1, has_up & has_left), (17, 1, has_up & has_right),
        (18, 1, has_down & has_left), (19, 1, has_down & has_right),
    ))
    spread = others[sides_at:] + jnp.dot(
        g_halo[sides_at:, 256:384], normed[16:24].reshape(128, CHANS), preferred_element_type=F32
    )
    for at, (p, q) in enumerate(CORNER_TILES):
        cells[p, q] = spread[at * 16 : (at + 1) * 16].astype(BF16)
    convolve_rest(cells, k1, acc, CORNER_TILES)

    value = joined(acc, 5, 5)
    value = value / (1.0 + jnp.exp(-value))
    def flag(there):
        return jnp.where(there, 1.0, 0.0).astype(F32)

    j_of = lax.broadcasted_iota(jnp.int32, (1, 8, CHANS), 1) % 2
    sides = jnp.where(j_of == 0, flag(has_left), flag(has_right))
    inner, below = value[0:4], value[4]
    top = jnp.stack([below[:, 0] * flag(has_up), inner[3][:, 0]], axis=1)
    bottom = jnp.stack([inner[0][:, 1], below[:, 1] * flag(has_down)], axis=1)
    for p, line in enumerate((top, inner[0], inner[1], inner[2], inner[3], bottom)):
        edge = line[4] * sides
        first = jnp.where(j_of == 0, edge, pltpu.roll(line[3], 1, 1))
        last = jnp.where(j_of == 1, edge, pltpu.roll(line[0], 7, 1))
        for q, tile in enumerate((first, line[0], line[1], line[2], line[3], last)):
            hidden[p, q] = tile.reshape(16, CHANS).astype(BF16)

    load_k2.wait()

    def mix(half):
        convolve(hidden, k2, acc, half)
        before = kept[128 * half : 128 * half + 128].reshape(2, 4, 2, 8, CHANS)
        mixed = (before + joined(acc, 2, 4)).astype(BF16).reshape(8, 16, CHANS)
        for tile in range(8):
            lat[8 * half + tile, zh, y] = mixed[tile]

    zs = [zh] + [lax.rem(zh + step, RING) for step in (1, 2, 3)]
    ys = [y] + [lax.rem(y + step, RING) for step in (1, 2, 3)]
    pending = []
    near, far, near2, far2 = {}, {}, {}, {}

    def pieces(c, u, v, part=None):
        first, last, y_first = PARTS[c]
        if part is not None:
            middle = (first + last) // 2
            first, last = (first, middle) if part == 0 else (middle, last)
        a, b = (zs[v], ys[u]) if y_first else (zs[u], ys[v])
        return lat.at[pl.ds(first, last - first), a, b]

    def straight(c, u):
        return any(move == "D%d%d" % (c, u) for move in ORDER)

    def pass_on(piece, send_sem, recv_sem, device):
        copy = send(piece, piece, send_sem, recv_sem, device)
        pending.append(copy)
        return copy

    def multiply(c, which, taps):
        first, last, y_first = PARTS[c]
        for b in taps:
            part = None
            for tile in range(first, last):
                block = jnp.concatenate(
                    [(lat[tile, :, ys[u]] if y_first else lat[tile, zs[u]]).reshape(64, CHANS) for u in which], axis=0
                )
                term = lax.dot_general(
                    block,
                    w[b, :, tile * CHANS : (tile + 1) * CHANS],
                    (((1,), (1,)), ((), ())),
                    preferred_element_type=F32,
                )
                part = term if part is None else part + term
            for at, u in enumerate(which):
                term = part[at * 64 : (at + 1) * 64].reshape(RING, 16, 3 * OUT_DEV)
                if y_first:
                    y_acc[b, :, ys[u]] += term
                else:
                    y_acc[b, zs[u]] += term

    for move in ORDER:
        what, c, u = move[0], int(move[1]), int(move[2:3] or 0)
        if what == "C":
            mix(c)
            continue
        rings = (to_y, to_z) if PARTS[c][2] else (to_z, to_y)
        opposite = (to_y2, to_z2) if PARTS[c][2] else (to_z2, to_y2)
        if what == "n":
            near[c] = [
                pass_on(pieces(c, 0, 0), near_send.at[c, d], near_recv.at[c, d], rings[0][d]) for d in range(2)
            ]
        elif what == "f":
            for copy in near[c]:
                copy.wait_recv()
            far[c] = [
                pass_on(pieces(c, 3 - 2 * d, 0, d), far_send.at[c, d], far_recv.at[c, d], rings[0][d]) for d in range(2)
            ]
        elif what == "d":
            far[c] = [pass_on(pieces(c, 0, 0), far_send.at[c, 0], far_recv.at[c, 0], opposite[0])]
        elif what == "e":
            for copy in near[c]:
                copy.wait_recv()
        elif what in "ND":
            if u == 2:
                for copy in far[c]:
                    copy.wait_recv()
            near2[c, u] = [
                pass_on(pieces(c, u, 0), near2_send.at[c, u, d], near2_recv.at[c, u, d], rings[1][d]) for d in range(2)
            ]
            if what == "D":
                far2[c, u] = pass_on(pieces(c, u, 0), far2_send.at[c, u], far2_recv.at[c, u], opposite[1])
        elif what == "F":
            for copy in near2[c, u]:
                copy.wait_recv()
            d = (0, 1, 1, 0)[u] if c % 2 == 0 else (1, 1, 0, 0)[u]
            far2[c, u] = pass_on(pieces(c, u, 3 - 2 * d), far2_send.at[c, u], far2_recv.at[c, u], rings[1][d])
        else:
            for copy in w_loads:
                copy.wait()
            w_loads = []
            which = [int(u) for u in move[2:]]
            for u in which:
                if straight(c, u):
                    for copy in near2[c, u]:
                        copy.wait_recv()
                far2[c, u].wait_recv()
            multiply(c, which, (0, 2))

    s = lax.broadcasted_iota(jnp.int32, (1, 16, OUT_DEV), 1) % 2
    edge = jnp.zeros((1, 16, OUT_DEV), F32)

    def moved(b):
        sums = y_acc[b].reshape(PIECES, 16, 3 * OUT_DEV)
        first, second, third = (sums[..., e * OUT_DEV : (e + 1) * OUT_DEV] for e in range(3))
        from_left = jnp.concatenate([edge, pltpu.roll(first, 15, 1)[: PIECES - 1]], axis=0)
        from_right = jnp.concatenate([pltpu.roll(third, 1, 1)[1:], edge], axis=0)
        total = second + jnp.where(s == 1, pltpu.roll(first, 1, 1), from_left)
        total += jnp.where(s == 0, pltpu.roll(third, 15, 1), from_right)
        return total.reshape(PIECES, 2, 8, OUT_DEV)

    def pack(part):
        return jnp.concatenate([part[:8].reshape(64, OUT_DEV), part[8:].reshape(64, OUT_DEV)], axis=1)

    above, below = moved(0), moved(2)
    u_out[0] = pack(below[:, 0])
    u_out[1] = pack(above[:, 1])
    rows_sent = [
        send(u_out.at[0], u_in.at[1], u_send.at[0], u_recv.at[0], (up, col)),
        send(u_out.at[1], u_in.at[0], u_send.at[1], u_recv.at[1], (down, col)),
    ]
    for c in range(CHUNKS):
        multiply(c, range(RING), (1,))
    load_mean.wait()
    centre = lat[col].reshape(256, CHANS)
    shortcut = jnp.dot(centre, g_mean[...], preferred_element_type=F32).reshape(PIECES, 2, 8, OUT_DEV)
    same = moved(1) + shortcut
    result0 = same[:, 0] + below[:, 1]
    result1 = same[:, 1] + above[:, 0]

    for copy in rows_sent:
        copy.wait_recv()

    def unpack(part, there):
        part = jnp.where(there, part, 0.0)
        return jnp.concatenate(
            [part[:, :OUT_DEV].reshape(8, 8, OUT_DEV), part[:, OUT_DEV:].reshape(8, 8, OUT_DEV)], axis=0
        )

    out_ref[0] = (result0 + unpack(u_in[0], has_up)).reshape(128, OUT_DEV).astype(BF16)
    out_ref[1] = (result1 + unpack(u_in[1], has_down)).reshape(128, OUT_DEV).astype(BF16)
    for copy in sent + pending + rows_sent:
        copy.wait_send()


def per_device(n_row, n_col, frames_in, norm_gain, first_kernel, second_kernel, latent_kernel):
    g_own, g_halo = spread_tables()
    anywhere = pl.BlockSpec(memory_space=pltpu.HBM)
    dma = pltpu.SemaphoreType.DMA
    out = pl.pallas_call(
        functools.partial(kernel, n_row, n_col),
        out_shape=jax.ShapeDtypeStruct((2, 128, OUT_DEV), BF16),
        in_specs=[anywhere] * 9,
        out_specs=pl.BlockSpec(memory_space=pltpu.VMEM),
        scratch_shapes=[
            pltpu.VMEM((4, 4, 16, CHANS), BF16),
            pltpu.VMEM((1, CHANS), F32),
            pltpu.VMEM((3, 3, 3, CHANS, CHANS), BF16),
            pltpu.VMEM((3, 3, 3, CHANS, CHANS), BF16),
            pltpu.VMEM((3, 3 * OUT_DEV, LATENT), BF16),
            pltpu.VMEM((81 * 16, 256), BF16),
            pltpu.VMEM((65 * 16, 384), BF16),
            pltpu.VMEM((128, 256), BF16),
            pltpu.VMEM((CHANS, OUT_DEV), BF16),
            pltpu.VMEM((2, 4, 16, CHANS), BF16),
            pltpu.VMEM((20, 16, CHANS), BF16),
            pltpu.VMEM((24, 16, CHANS), BF16),
            pltpu.VMEM((9, 9, 16, CHANS), BF16),
            pltpu.VMEM((65 * 16, CHANS), F32),
            pltpu.VMEM((6, 6, 16, CHANS), BF16),
            pltpu.VMEM((3, 5, 5, 16, CHANS), F32),
            pltpu.VMEM((PIECES, RING, RING, 16, CHANS), BF16),
            pltpu.VMEM((3, RING, RING, 16, 3 * OUT_DEV), F32),
            pltpu.VMEM((2, 64, 2 * OUT_DEV), F32),
            pltpu.VMEM((2, 64, 2 * OUT_DEV), F32),
            pltpu.VMEM((256, CHANS), F32),
            dma((8,)),
            dma((3,)),
            dma((8,)),
            dma((8,)),
            dma((CHUNKS, 2)),
            dma((CHUNKS, 2)),
            dma((CHUNKS, 2)),
            dma((CHUNKS, 2)),
            dma((CHUNKS, RING, 2)),
            dma((CHUNKS, RING, 2)),
            dma((CHUNKS, RING)),
            dma((CHUNKS, RING)),
            dma((2,)),
            dma((2,)),
        ],
        compiler_params=pltpu.CompilerParams(
            collective_id=0, has_side_effects=True, vmem_limit_bytes=60 << 20
        ),
        cost_estimate=pl.CostEstimate(flops=4 << 30, bytes_accessed=14 << 20, transcendentals=1 << 18),
    )(
        frames_in.reshape(4, 4, 16, CHANS),
        norm_gain.reshape(1, CHANS),
        first_kernel,
        second_kernel,
        latent_kernel.transpose(0, 1, 3, 2).reshape(3, 3 * OUT_DEV, LATENT),
        g_own,
        g_halo,
        strip_table(),
        mean_table(),
    )
    out = out.reshape(2, PIECES, FRAMES, 2, OUT_DEV)
    return out.transpose(2, 0, 1, 3, 4).reshape(FRAMES, 2, 2 * PIECES, OUT_DEV)


def solution(mesh):
    return jax.shard_map(
        functools.partial(per_device, mesh.shape["row"], mesh.shape["col"]),
        mesh=mesh,
        in_specs=(P(None, "row", "col", None), P(), P(), P(), P(None, None, None, "col")),
        out_specs=P(None, "row", None, "col"),
        check_vma=False,
    )
```

```python
import functools

import jax
import jax.numpy as jnp
import numpy as np
from jax import lax
from jax.experimental import pallas as pl
from jax.experimental.pallas import tpu as pltpu
from jax.sharding import PartitionSpec as P

MESH = pl.DeviceIdType.MESH
F32 = jnp.float32
BF16 = jnp.bfloat16
FRAMES, SIDE, CHANS = 4, 8, 256
OUT_CH, LATENT = 1024, 4096
RING = 4
PIECES = RING * RING
OUT_DEV = OUT_CH // PIECES
PARTS = ((0, 6, False), (6, 12, False), (12, 16, True))
CHUNKS = len(PARTS)
ORDER = (
    ("C0", "n0", "N00", "C1", "n2", "d2", "n1", "N10", "f0", "N01", "N03", "f1", "N11", "N13", "e2", "N20", "N21", "N23", "N22")
    + ("F00", "F10", "D02", "D12", "F01", "F03", "F11", "F13", "F20", "F21", "F23", "F22", "W00132", "W10132", "W20132")
)


def one_hot(index, width):
    out = np.zeros((len(index), width), np.float32)
    for at, source in enumerate(index):
        if source >= 0:
            out[at, source] = 1
    return out.astype(BF16)


OWN_TILES = [(p, q) for p in range(1, 5) for q in range(1, 5)]
CORNER_TILES = [(p, q) for p in (0, 5, 6, 7, 8) for q in (0, 5, 6, 7, 8)]
SIDE_TILES = [(p, q) for p in range(9) for q in range(9) if (p, q) not in OWN_TILES + CORNER_TILES]


def line_of(tile, half):
    if tile < 6:
        return 4 * half + tile - 1
    return tile - 6 + (7 if half else -2)


def spread_tables():
    own, halo = [], []
    for p, q in OWN_TILES + SIDE_TILES + CORNER_TILES:
        for i in range(2):
            for f in range(FRAMES):
                for j in range(2):
                    r, c = line_of(p, i), line_of(q, j)
                    inside_r, inside_c = 0 <= r < SIDE, 0 <= c < SIDE
                    a, b = -1, -1
                    side = 0 if c < 0 else 1
                    cc = c + 2 if c < 0 else c - SIDE
                    rr = r + 2 if r < 0 else r - SIDE
                    if inside_r and inside_c:
                        a = f * 64 + r * 8 + c
                    elif inside_c:
                        b = ((0 if r < 0 else 4) + f) * 16 + rr * 8 + c
                    elif inside_r:
                        b = (8 + 4 * side + r // 2) * 16 + f * 4 + (r % 2) * 2 + cc
                    else:
                        b = (16 + (0 if r < 0 else 2) + side) * 16 + f * 4 + rr * 2 + cc
                    own.append(a)
                    halo.append(b)
    return one_hot(own, 256), one_hot(halo[256:], 384)


def strip_table():
    index = []
    for side in range(2):
        for rp in range(4):
            for f in range(FRAMES):
                for rr in range(2):
                    for cc in range(2):
                        index.append(f * 64 + (2 * rp + rr) * 8 + 6 * side + cc)
    return one_hot(index, 256)


def mean_table():
    group = LATENT // OUT_CH
    out = np.zeros((CHANS, CHANS // group), np.float32)
    out[np.arange(CHANS), np.arange(CHANS) // group] = 1 / group
    return out.astype(BF16)


def convolve_own(cells, w, acc):
    acc[:, 4] = jnp.zeros((3, 5, 16, CHANS), F32)
    acc[:, 0:4, 4] = jnp.zeros((3, 4, 16, CHANS), F32)
    order = [(1, 1)] + [(b, e) for b in range(3) for e in range(3) if (b, e) != (1, 1)]
    for a in range(3):
        for b, e in order:
            p0, p1, q0, q1 = max(0, 1 - b), min(4, 5 - b), max(0, 1 - e), min(4, 5 - e)
            shape = (p1 - p0, q1 - q0, 16, CHANS)
            lhs = cells[p0 + b : p1 + b, q0 + e : q1 + e].reshape(-1, CHANS)
            part = jnp.dot(lhs, w[a, b, e], preferred_element_type=F32).reshape(shape)
            if (b, e) == (1, 1):
                acc[a, 0:4, 0:4] = part
            else:
                acc[a, p0:p1, q0:q1] += part


def convolve_rest(cells, w, acc, sources):
    for a in range(3):
        for b in range(3):
            for e in range(3):
                reads = {
                    (p, q): (p + b if p < 4 else 6 + b, q + e if q < 4 else 6 + e) for p in range(5) for q in range(5)
                }
                tiles = [tile for tile in reads if reads[tile] in sources]
                lhs = jnp.concatenate([cells[reads[tile]] for tile in tiles], axis=0)
                part = jnp.dot(lhs, w[a, b, e], preferred_element_type=F32)
                for at, (p, q) in enumerate(tiles):
                    acc[a, p, q] += part[at * 16 : (at + 1) * 16]


def convolve(src, w, acc, half):
    for a in range(3):
        total = None
        for b in range(3):
            for e in range(3):
                lhs = src[2 * half + b : 2 * half + b + 2, e : e + 4].reshape(128, CHANS)
                part = jnp.dot(lhs, w[a, b, e], preferred_element_type=F32)
                total = part if total is None else total + part
        acc[a, 0:2, 0:4] = total.reshape(2, 4, 16, CHANS)


def joined(acc, m, n):
    early, same, late = (acc[a, 0:m, 0:n].reshape(m * n * 2, 8, CHANS) for a in range(3))
    f = lax.broadcasted_iota(jnp.int32, (1, 8, CHANS), 1) // 2
    total = same + jnp.where(f > 0, pltpu.roll(early, 2, 1), 0.0)
    total += jnp.where(f < FRAMES - 1, pltpu.roll(late, 6, 1), 0.0)
    return total.reshape(m, n, 2, 8, CHANS)


def kernel(
    n_row, n_col,
    x_hbm, gain_hbm, k1_hbm, k2_hbm, w_hbm, g_own_hbm, g_halo_hbm, g_strip_hbm, g_mean_hbm,
    out_ref,
    x, gain, k1, k2, w, g_own, g_halo, g_strip, g_mean,
    strips, halo, normed, cells, others, hidden, acc, lat, y_acc, u_out, u_in, kept,
    load_sem, w_sem, halo_send, halo_recv,
    near_send, near_recv, far_send, far_recv, near2_send, near2_recv, far2_send, far2_recv,
    u_send, u_recv,
):
    row, col = lax.axis_index("row"), lax.axis_index("col")
    zh, y = col // RING, col % RING
    up, down = lax.rem(row + n_row - 1, n_row), lax.rem(row + 1, n_row)
    left, right = lax.rem(col + n_col - 1, n_col), lax.rem(col + 1, n_col)
    z_next, z_prev = lax.rem(zh + 1, RING), lax.rem(zh + RING - 1, RING)
    y_next, y_prev = lax.rem(y + 1, RING), lax.rem(y + RING - 1, RING)
    to_z = ((row, z_next * RING + y), (row, z_prev * RING + y))
    to_y = ((row, zh * RING + y_next), (row, zh * RING + y_prev))

    to_z2 = (row, lax.rem(zh + 2, RING) * RING + y)
    to_y2 = (row, zh * RING + lax.rem(y + 2, RING))

    barrier = pltpu.get_barrier_semaphore()
    around = (
        (up, left), (up, right), (down, left), (down, right),
        (up, col), (down, col), (row, left), (row, right),
    ) + to_z + to_y + (to_z2, to_y2)
    for target in around:
        pl.semaphore_signal(barrier, inc=1, device_id=target, device_id_type=MESH)

    loads = []
    for at, (source, target) in enumerate((
        (x_hbm, x), (g_strip_hbm, g_strip), (gain_hbm, gain), (g_own_hbm, g_own), (k1_hbm, k1),
        (g_halo_hbm, g_halo), (k2_hbm, k2), (g_mean_hbm, g_mean),
    )):
        copy = pltpu.make_async_copy(source, target, load_sem.at[at])
        copy.start()
        loads.append(copy)
    w_loads = []
    for b in range(3):
        copy = pltpu.make_async_copy(w_hbm.at[b], w.at[b], w_sem.at[b])
        copy.start()
        w_loads.append(copy)
    load_x, load_strip, load_gain, load_own, load_k1, load_halo, load_k2, load_mean = loads

    def send(source, target, send_sem, recv_sem, device):
        copy = pltpu.make_async_remote_copy(
            src_ref=source, dst_ref=target, send_sem=send_sem, recv_sem=recv_sem, device_id=device, device_id_type=MESH
        )
        copy.start()
        return copy

    load_x.wait()
    load_strip.wait()
    own = x[...].reshape(256, CHANS)
    strips[...] = jnp.dot(g_strip[...], own, preferred_element_type=F32).astype(BF16).reshape(2, 4, 16, CHANS)
    pl.semaphore_wait(barrier, len(around))
    sent = [
        send(strips.at[0, 3], halo.at[17], halo_send.at[4], halo_recv.at[4], (down, left)),
        send(strips.at[1, 3], halo.at[16], halo_send.at[5], halo_recv.at[5], (down, right)),
        send(strips.at[0, 0], halo.at[19], halo_send.at[6], halo_recv.at[6], (up, left)),
        send(strips.at[1, 0], halo.at[18], halo_send.at[7], halo_recv.at[7], (up, right)),
        send(x.at[:, 0], halo.at[pl.ds(4, 4)], halo_send.at[0], halo_recv.at[0], (up, col)),
        send(x.at[:, 3], halo.at[pl.ds(0, 4)], halo_send.at[1], halo_recv.at[1], (down, col)),
        send(strips.at[0], halo.at[pl.ds(12, 4)], halo_send.at[2], halo_recv.at[2], (row, left)),
        send(strips.at[1], halo.at[pl.ds(8, 4)], halo_send.at[3], halo_recv.at[3], (row, right)),
    ]

    load_gain.wait()

    def norm(raw):
        values = raw.astype(F32)
        scale = lax.rsqrt(jnp.mean(values * values, axis=-1, keepdims=True) + 1e-06)
        return values * scale * gain[...]

    own_normed = norm(own).astype(BF16)
    normed[20:24] = jnp.zeros((4, 16, CHANS), BF16)
    y_acc[...] = jnp.zeros(y_acc.shape, F32)
    load_own.wait()
    middle = jnp.dot(g_own[0:256], own_normed, preferred_element_type=F32)
    cells[1:5, 1:5] = middle.astype(BF16).reshape(4, 4, 16, CHANS)
    load_k1.wait()
    convolve_own(cells, k1, acc)
    others[...] = jnp.dot(g_own[256:], own_normed, preferred_element_type=F32)
    kept[...] = jnp.dot(g_own[0:256], own, preferred_element_type=F32)
    load_halo.wait()

    has_up, has_down = row > 0, row < n_row - 1
    has_left, has_right = col > 0, col < n_col - 1

    def norm_halo(parts):
        for start, count, there in parts:
            values = norm(halo[start : start + count].reshape(count * 16, CHANS))
            values = values * jnp.where(there, 1.0, 0.0).astype(F32)
            normed[start : start + count] = values.astype(BF16).reshape(count, 16, CHANS)

    sides_at = 16 * len(SIDE_TILES)
    for copy in sent[4:]:
        copy.wait_recv()
    norm_halo(((0, 4, has_up), (4, 4, has_down), (8, 4, has_left), (12, 4, has_right)))
    spread = others[...] + jnp.dot(
        g_halo[:, 0:256], normed[0:16].reshape(256, CHANS), preferred_element_type=F32
    )
    for at, (p, q) in enumerate(SIDE_TILES):
        cells[p, q] = spread[at * 16 : (at + 1) * 16].astype(BF16)
    others[sides_at:] = spread[sides_at:]
    convolve_rest(cells, k1, acc, SIDE_TILES)

    for copy in sent[:4]:
        copy.wait_recv()
    norm_halo((
        (16, 1, has_up & has_left), (17, 1, has_up & has_right),
        (18, 1, has_down & has_left), (19, 1, has_down & has_right),
    ))
    spread = others[sides_at:] + jnp.dot(
        g_halo[sides_at:, 256:384], normed[16:24].reshape(128, CHANS), preferred_element_type=F32
    )
    for at, (p, q) in enumerate(CORNER_TILES):
        cells[p, q] = spread[at * 16 : (at + 1) * 16].astype(BF16)
    convolve_rest(cells, k1, acc, CORNER_TILES)

    value = joined(acc, 5, 5)
    value = value / (1.0 + jnp.exp(-value))
    def flag(there):
        return jnp.where(there, 1.0, 0.0).astype(F32)

    j_of = lax.broadcasted_iota(jnp.int32, (1, 8, CHANS), 1) % 2
    sides = jnp.where(j_of == 0, flag(has_left), flag(has_right))
    inner, below = value[0:4], value[4]
    top = jnp.stack([below[:, 0] * flag(has_up), inner[3][:, 0]], axis=1)
    bottom = jnp.stack([inner[0][:, 1], below[:, 1] * flag(has_down)], axis=1)
    for p, line in enumerate((top, inner[0], inner[1], inner[2], inner[3], bottom)):
        edge = line[4] * sides
        first = jnp.where(j_of == 0, edge, pltpu.roll(line[3], 1, 1))
        last = jnp.where(j_of == 1, edge, pltpu.roll(line[0], 7, 1))
        for q, tile in enumerate((first, line[0], line[1], line[2], line[3], last)):
            hidden[p, q] = tile.reshape(16, CHANS).astype(BF16)

    load_k2.wait()

    def mix(half):
        convolve(hidden, k2, acc, half)
        before = kept[128 * half : 128 * half + 128].reshape(2, 4, 2, 8, CHANS)
        mixed = (before + joined(acc, 2, 4)).astype(BF16).reshape(8, 16, CHANS)
        for tile in range(8):
            lat[8 * half + tile, zh, y] = mixed[tile]

    zs = [zh] + [lax.rem(zh + step, RING) for step in (1, 2, 3)]
    ys = [y] + [lax.rem(y + step, RING) for step in (1, 2, 3)]
    pending = []
    near, far, near2, far2 = {}, {}, {}, {}

    def pieces(c, u, v, part=None):
        first, last, y_first = PARTS[c]
        if part is not None:
            middle = (first + last) // 2
            first, last = (first, middle) if part == 0 else (middle, last)
        a, b = (zs[v], ys[u]) if y_first else (zs[u], ys[v])
        return lat.at[pl.ds(first, last - first), a, b]

    def straight(c, u):
        return any(move == "D%d%d" % (c, u) for move in ORDER)

    def pass_on(piece, send_sem, recv_sem, device):
        copy = send(piece, piece, send_sem, recv_sem, device)
        pending.append(copy)
        return copy

    def multiply(c, which, taps):
        first, last, y_first = PARTS[c]
        for b in taps:
            part = None
            for tile in range(first, last):
                block = jnp.concatenate(
                    [(lat[tile, :, ys[u]] if y_first else lat[tile, zs[u]]).reshape(64, CHANS) for u in which], axis=0
                )
                term = lax.dot_general(
                    block,
                    w[b, :, tile * CHANS : (tile + 1) * CHANS],
                    (((1,), (1,)), ((), ())),
                    preferred_element_type=F32,
                )
                part = term if part is None else part + term
            for at, u in enumerate(which):
                term = part[at * 64 : (at + 1) * 64].reshape(RING, 16, 3 * OUT_DEV)
                if y_first:
                    y_acc[b, :, ys[u]] += term
                else:
                    y_acc[b, zs[u]] += term

    for move in ORDER:
        what, c, u = move[0], int(move[1]), int(move[2:3] or 0)
        if what == "C":
            mix(c)
            continue
        rings = (to_y, to_z) if PARTS[c][2] else (to_z, to_y)
        opposite = (to_y2, to_z2) if PARTS[c][2] else (to_z2, to_y2)
        if what == "n":
            near[c] = [
                pass_on(pieces(c, 0, 0), near_send.at[c, d], near_recv.at[c, d], rings[0][d]) for d in range(2)
            ]
        elif what == "f":
            for copy in near[c]:
                copy.wait_recv()
            far[c] = [
                pass_on(pieces(c, 3 - 2 * d, 0, d), far_send.at[c, d], far_recv.at[c, d], rings[0][d]) for d in range(2)
            ]
        elif what == "d":
            far[c] = [pass_on(pieces(c, 0, 0), far_send.at[c, 0], far_recv.at[c, 0], opposite[0])]
        elif what == "e":
            for copy in near[c]:
                copy.wait_recv()
        elif what in "ND":
            if u == 2:
                for copy in far[c]:
                    copy.wait_recv()
            near2[c, u] = [
                pass_on(pieces(c, u, 0), near2_send.at[c, u, d], near2_recv.at[c, u, d], rings[1][d]) for d in range(2)
            ]
            if what == "D":
                far2[c, u] = pass_on(pieces(c, u, 0), far2_send.at[c, u], far2_recv.at[c, u], opposite[1])
        elif what == "F":
            for copy in near2[c, u]:
                copy.wait_recv()
            d = (0, 1, 1, 0)[u] if c % 2 == 0 else (1, 1, 0, 0)[u]
            far2[c, u] = pass_on(pieces(c, u, 3 - 2 * d), far2_send.at[c, u], far2_recv.at[c, u], rings[1][d])
        else:
            for copy in w_loads:
                copy.wait()
            w_loads = []
            which = [int(u) for u in move[2:]]
            for u in which:
                if straight(c, u):
                    for copy in near2[c, u]:
                        copy.wait_recv()
                far2[c, u].wait_recv()
            multiply(c, which, (0, 2))

    s = lax.broadcasted_iota(jnp.int32, (1, 16, OUT_DEV), 1) % 2
    edge = jnp.zeros((1, 16, OUT_DEV), F32)

    def moved(b):
        sums = y_acc[b].reshape(PIECES, 16, 3 * OUT_DEV)
        first, second, third = (sums[..., e * OUT_DEV : (e + 1) * OUT_DEV] for e in range(3))
        from_left = jnp.concatenate([edge, pltpu.roll(first, 15, 1)[: PIECES - 1]], axis=0)
        from_right = jnp.concatenate([pltpu.roll(third, 1, 1)[1:], edge], axis=0)
        total = second + jnp.where(s == 1, pltpu.roll(first, 1, 1), from_left)
        total += jnp.where(s == 0, pltpu.roll(third, 15, 1), from_right)
        return total.reshape(PIECES, 2, 8, OUT_DEV)

    def pack(part):
        return jnp.concatenate([part[:8].reshape(64, OUT_DEV), part[8:].reshape(64, OUT_DEV)], axis=1)

    above, below = moved(0), moved(2)
    u_out[0] = pack(below[:, 0])
    u_out[1] = pack(above[:, 1])
    rows_sent = [
        send(u_out.at[0], u_in.at[1], u_send.at[0], u_recv.at[0], (up, col)),
        send(u_out.at[1], u_in.at[0], u_send.at[1], u_recv.at[1], (down, col)),
    ]
    for c in range(CHUNKS):
        multiply(c, range(RING), (1,))
    load_mean.wait()
    centre = lat[col].reshape(256, CHANS)
    shortcut = jnp.dot(centre, g_mean[...], preferred_element_type=F32).reshape(PIECES, 2, 8, OUT_DEV)
    same = moved(1) + shortcut
    result0 = same[:, 0] + below[:, 1]
    result1 = same[:, 1] + above[:, 0]

    for copy in rows_sent:
        copy.wait_recv()

    def unpack(part, there):
        part = jnp.where(there, part, 0.0)
        return jnp.concatenate(
            [part[:, :OUT_DEV].reshape(8, 8, OUT_DEV), part[:, OUT_DEV:].reshape(8, 8, OUT_DEV)], axis=0
        )

    out_ref[0] = (result0 + unpack(u_in[0], has_up)).reshape(128, OUT_DEV).astype(BF16)
    out_ref[1] = (result1 + unpack(u_in[1], has_down)).reshape(128, OUT_DEV).astype(BF16)
    for copy in sent + pending + rows_sent:
        copy.wait_send()


def per_device(n_row, n_col, frames_in, norm_gain, first_kernel, second_kernel, latent_kernel):
    g_own, g_halo = spread_tables()
    anywhere = pl.BlockSpec(memory_space=pltpu.HBM)
    dma = pltpu.SemaphoreType.DMA
    out = pl.pallas_call(
        functools.partial(kernel, n_row, n_col),
        out_shape=jax.ShapeDtypeStruct((2, 128, OUT_DEV), BF16),
        in_specs=[anywhere] * 9,
        out_specs=pl.BlockSpec(memory_space=pltpu.VMEM),
        scratch_shapes=[
            pltpu.VMEM((4, 4, 16, CHANS), BF16),
            pltpu.VMEM((1, CHANS), F32),
            pltpu.VMEM((3, 3, 3, CHANS, CHANS), BF16),
            pltpu.VMEM((3, 3, 3, CHANS, CHANS), BF16),
            pltpu.VMEM((3, 3 * OUT_DEV, LATENT), BF16),
            pltpu.VMEM((81 * 16, 256), BF16),
            pltpu.VMEM((65 * 16, 384), BF16),
            pltpu.VMEM((128, 256), BF16),
            pltpu.VMEM((CHANS, OUT_DEV), BF16),
            pltpu.VMEM((2, 4, 16, CHANS), BF16),
            pltpu.VMEM((20, 16, CHANS), BF16),
            pltpu.VMEM((24, 16, CHANS), BF16),
            pltpu.VMEM((9, 9, 16, CHANS), BF16),
            pltpu.VMEM((65 * 16, CHANS), F32),
            pltpu.VMEM((6, 6, 16, CHANS), BF16),
            pltpu.VMEM((3, 5, 5, 16, CHANS), F32),
            pltpu.VMEM((PIECES, RING, RING, 16, CHANS), BF16),
            pltpu.VMEM((3, RING, RING, 16, 3 * OUT_DEV), F32),
            pltpu.VMEM((2, 64, 2 * OUT_DEV), F32),
            pltpu.VMEM((2, 64, 2 * OUT_DEV), F32),
            pltpu.VMEM((256, CHANS), F32),
            dma((8,)),
            dma((3,)),
            dma((8,)),
            dma((8,)),
            dma((CHUNKS, 2)),
            dma((CHUNKS, 2)),
            dma((CHUNKS, 2)),
            dma((CHUNKS, 2)),
            dma((CHUNKS, RING, 2)),
            dma((CHUNKS, RING, 2)),
            dma((CHUNKS, RING)),
            dma((CHUNKS, RING)),
            dma((2,)),
            dma((2,)),
        ],
        compiler_params=pltpu.CompilerParams(
            collective_id=0, has_side_effects=True, vmem_limit_bytes=60 << 20
        ),
        cost_estimate=pl.CostEstimate(flops=4 << 30, bytes_accessed=14 << 20, transcendentals=1 << 18),
    )(
        frames_in.reshape(4, 4, 16, CHANS),
        norm_gain.reshape(1, CHANS),
        first_kernel,
        second_kernel,
        latent_kernel.transpose(0, 1, 3, 2).reshape(3, 3 * OUT_DEV, LATENT),
        g_own,
        g_halo,
        strip_table(),
        mean_table(),
    )
    out = out.reshape(2, PIECES, FRAMES, 2, OUT_DEV)
    return out.transpose(2, 0, 1, 3, 4).reshape(FRAMES, 2, 2 * PIECES, OUT_DEV)


def solution(mesh):
    return jax.shard_map(
        functools.partial(per_device, mesh.shape["row"], mesh.shape["col"]),
        mesh=mesh,
        in_specs=(P(None, "row", "col", None), P(), P(), P(), P(None, None, None, "col")),
        out_specs=P(None, "row", None, "col"),
        check_vma=False,
    )
```

```python
import functools

import jax
import jax.numpy as jnp
import numpy as np
from jax import lax
from jax.experimental import pallas as pl
from jax.experimental.pallas import tpu as pltpu
from jax.sharding import PartitionSpec as P

MESH = pl.DeviceIdType.MESH
F32 = jnp.float32
BF16 = jnp.bfloat16
FRAMES, SIDE, CHANS = 4, 8, 256
OUT_CH, LATENT = 1024, 4096
RING = 4
PIECES = RING * RING
OUT_DEV = OUT_CH // PIECES
PARTS = ((0, 6, False), (6, 12, False), (12, 16, True))
CHUNKS = len(PARTS)
ORDER = (
    ("C0", "n0", "N00", "C1", "n1", "n2", "d2", "N10", "e2", "f0", "N01", "N03", "f1", "N11", "N13", "N20", "N21", "N23", "N22")
    + ("F00", "F10", "D02", "D12", "F01", "F03", "F11", "F13", "F20", "F21", "F23", "F22", "W00132", "W10132", "W20132")
)


def one_hot(index, width):
    out = np.zeros((len(index), width), np.float32)
    for at, source in enumerate(index):
        if source >= 0:
            out[at, source] = 1
    return out.astype(BF16)


OWN_TILES = [(p, q) for p in range(1, 5) for q in range(1, 5)]
CORNER_TILES = [(p, q) for p in (0, 5, 6, 7, 8) for q in (0, 5, 6, 7, 8)]
SIDE_TILES = [(p, q) for p in range(9) for q in range(9) if (p, q) not in OWN_TILES + CORNER_TILES]


def line_of(tile, half):
    if tile < 6:
        return 4 * half + tile - 1
    return tile - 6 + (7 if half else -2)


def spread_tables():
    own, halo = [], []
    for p, q in OWN_TILES + SIDE_TILES + CORNER_TILES:
        for i in range(2):
            for f in range(FRAMES):
                for j in range(2):
                    r, c = line_of(p, i), line_of(q, j)
                    inside_r, inside_c = 0 <= r < SIDE, 0 <= c < SIDE
                    a, b = -1, -1
                    side = 0 if c < 0 else 1
                    cc = c + 2 if c < 0 else c - SIDE
                    rr = r + 2 if r < 0 else r - SIDE
                    if inside_r and inside_c:
                        a = f * 64 + r * 8 + c
                    elif inside_c:
                        b = ((0 if r < 0 else 4) + f) * 16 + rr * 8 + c
                    elif inside_r:
                        b = (8 + 4 * side + r // 2) * 16 + f * 4 + (r % 2) * 2 + cc
                    else:
                        b = (16 + (0 if r < 0 else 2) + side) * 16 + f * 4 + rr * 2 + cc
                    own.append(a)
                    halo.append(b)
    return one_hot(own, 256), one_hot(halo[256:], 384)


def strip_table():
    index = []
    for side in range(2):
        for rp in range(4):
            for f in range(FRAMES):
                for rr in range(2):
                    for cc in range(2):
                        index.append(f * 64 + (2 * rp + rr) * 8 + 6 * side + cc)
    return one_hot(index, 256)


def mean_table():
    group = LATENT // OUT_CH
    out = np.zeros((CHANS, CHANS // group), np.float32)
    out[np.arange(CHANS), np.arange(CHANS) // group] = 1 / group
    return out.astype(BF16)


def convolve_own(cells, w, acc):
    acc[:, 4] = jnp.zeros((3, 5, 16, CHANS), F32)
    acc[:, 0:4, 4] = jnp.zeros((3, 4, 16, CHANS), F32)
    order = [(1, 1)] + [(b, e) for b in range(3) for e in range(3) if (b, e) != (1, 1)]
    for a in range(3):
        for b, e in order:
            p0, p1, q0, q1 = max(0, 1 - b), min(4, 5 - b), max(0, 1 - e), min(4, 5 - e)
            shape = (p1 - p0, q1 - q0, 16, CHANS)
            lhs = cells[p0 + b : p1 + b, q0 + e : q1 + e].reshape(-1, CHANS)
            part = jnp.dot(lhs, w[a, b, e], preferred_element_type=F32).reshape(shape)
            if (b, e) == (1, 1):
                acc[a, 0:4, 0:4] = part
            else:
                acc[a, p0:p1, q0:q1] += part


def convolve_rest(cells, w, acc, sources):
    for a in range(3):
        for b in range(3):
            for e in range(3):
                reads = {
                    (p, q): (p + b if p < 4 else 6 + b, q + e if q < 4 else 6 + e) for p in range(5) for q in range(5)
                }
                tiles = [tile for tile in reads if reads[tile] in sources]
                lhs = jnp.concatenate([cells[reads[tile]] for tile in tiles], axis=0)
                part = jnp.dot(lhs, w[a, b, e], preferred_element_type=F32)
                for at, (p, q) in enumerate(tiles):
                    acc[a, p, q] += part[at * 16 : (at + 1) * 16]


def convolve(src, w, acc, half):
    for a in range(3):
        total = None
        for b in range(3):
            for e in range(3):
                lhs = src[2 * half + b : 2 * half + b + 2, e : e + 4].reshape(128, CHANS)
                part = jnp.dot(lhs, w[a, b, e], preferred_element_type=F32)
                total = part if total is None else total + part
        acc[a, 0:2, 0:4] = total.reshape(2, 4, 16, CHANS)


def joined(acc, m, n):
    early, same, late = (acc[a, 0:m, 0:n].reshape(m * n * 2, 8, CHANS) for a in range(3))
    f = lax.broadcasted_iota(jnp.int32, (1, 8, CHANS), 1) // 2
    total = same + jnp.where(f > 0, pltpu.roll(early, 2, 1), 0.0)
    total += jnp.where(f < FRAMES - 1, pltpu.roll(late, 6, 1), 0.0)
    return total.reshape(m, n, 2, 8, CHANS)


def kernel(
    n_row, n_col,
    x_hbm, gain_hbm, k1_hbm, k2_hbm, w_hbm, g_own_hbm, g_halo_hbm, g_strip_hbm, g_mean_hbm,
    out_ref,
    x, gain, k1, k2, w, g_own, g_halo, g_strip, g_mean,
    strips, halo, normed, cells, others, hidden, acc, lat, y_acc, u_out, u_in, kept,
    load_sem, w_sem, halo_send, halo_recv,
    near_send, near_recv, far_send, far_recv, near2_send, near2_recv, far2_send, far2_recv,
    u_send, u_recv,
):
    row, col = lax.axis_index("row"), lax.axis_index("col")
    zh, y = col // RING, col % RING
    up, down = lax.rem(row + n_row - 1, n_row), lax.rem(row + 1, n_row)
    left, right = lax.rem(col + n_col - 1, n_col), lax.rem(col + 1, n_col)
    z_next, z_prev = lax.rem(zh + 1, RING), lax.rem(zh + RING - 1, RING)
    y_next, y_prev = lax.rem(y + 1, RING), lax.rem(y + RING - 1, RING)
    to_z = ((row, z_next * RING + y), (row, z_prev * RING + y))
    to_y = ((row, zh * RING + y_next), (row, zh * RING + y_prev))

    to_z2 = (row, lax.rem(zh + 2, RING) * RING + y)
    to_y2 = (row, zh * RING + lax.rem(y + 2, RING))

    barrier = pltpu.get_barrier_semaphore()
    around = (
        (up, left), (up, right), (down, left), (down, right),
        (up, col), (down, col), (row, left), (row, right),
    ) + to_z + to_y + (to_z2, to_y2)
    for target in around:
        pl.semaphore_signal(barrier, inc=1, device_id=target, device_id_type=MESH)

    loads = []
    for at, (source, target) in enumerate((
        (x_hbm, x), (g_strip_hbm, g_strip), (gain_hbm, gain), (g_own_hbm, g_own), (k1_hbm, k1),
        (g_halo_hbm, g_halo), (k2_hbm, k2), (g_mean_hbm, g_mean),
    )):
        copy = pltpu.make_async_copy(source, target, load_sem.at[at])
        copy.start()
        loads.append(copy)
    w_loads = []
    for b in range(3):
        copy = pltpu.make_async_copy(w_hbm.at[b], w.at[b], w_sem.at[b])
        copy.start()
        w_loads.append(copy)
    load_x, load_strip, load_gain, load_own, load_k1, load_halo, load_k2, load_mean = loads

    def send(source, target, send_sem, recv_sem, device):
        copy = pltpu.make_async_remote_copy(
            src_ref=source, dst_ref=target, send_sem=send_sem, recv_sem=recv_sem, device_id=device, device_id_type=MESH
        )
        copy.start()
        return copy

    load_x.wait()
    load_strip.wait()
    own = x[...].reshape(256, CHANS)
    strips[...] = jnp.dot(g_strip[...], own, preferred_element_type=F32).astype(BF16).reshape(2, 4, 16, CHANS)
    pl.semaphore_wait(barrier, len(around))
    sent = [
        send(strips.at[0, 3], halo.at[17], halo_send.at[4], halo_recv.at[4], (down, left)),
        send(strips.at[1, 3], halo.at[16], halo_send.at[5], halo_recv.at[5], (down, right)),
        send(strips.at[0, 0], halo.at[19], halo_send.at[6], halo_recv.at[6], (up, left)),
        send(strips.at[1, 0], halo.at[18], halo_send.at[7], halo_recv.at[7], (up, right)),
        send(x.at[:, 0], halo.at[pl.ds(4, 4)], halo_send.at[0], halo_recv.at[0], (up, col)),
        send(x.at[:, 3], halo.at[pl.ds(0, 4)], halo_send.at[1], halo_recv.at[1], (down, col)),
        send(strips.at[0], halo.at[pl.ds(12, 4)], halo_send.at[2], halo_recv.at[2], (row, left)),
        send(strips.at[1], halo.at[pl.ds(8, 4)], halo_send.at[3], halo_recv.at[3], (row, right)),
    ]

    load_gain.wait()

    def norm(raw):
        values = raw.astype(F32)
        scale = lax.rsqrt(jnp.mean(values * values, axis=-1, keepdims=True) + 1e-06)
        return values * scale * gain[...]

    own_normed = norm(own).astype(BF16)
    normed[20:24] = jnp.zeros((4, 16, CHANS), BF16)
    y_acc[...] = jnp.zeros(y_acc.shape, F32)
    load_own.wait()
    middle = jnp.dot(g_own[0:256], own_normed, preferred_element_type=F32)
    cells[1:5, 1:5] = middle.astype(BF16).reshape(4, 4, 16, CHANS)
    load_k1.wait()
    convolve_own(cells, k1, acc)
    others[...] = jnp.dot(g_own[256:], own_normed, preferred_element_type=F32)
    kept[...] = jnp.dot(g_own[0:256], own, preferred_element_type=F32)
    load_halo.wait()

    has_up, has_down = row > 0, row < n_row - 1
    has_left, has_right = col > 0, col < n_col - 1

    def norm_halo(parts):
        for start, count, there in parts:
            values = norm(halo[start : start + count].reshape(count * 16, CHANS))
            values = values * jnp.where(there, 1.0, 0.0).astype(F32)
            normed[start : start + count] = values.astype(BF16).reshape(count, 16, CHANS)

    sides_at = 16 * len(SIDE_TILES)
    for copy in sent[4:]:
        copy.wait_recv()
    norm_halo(((0, 4, has_up), (4, 4, has_down), (8, 4, has_left), (12, 4, has_right)))
    spread = others[...] + jnp.dot(
        g_halo[:, 0:256], normed[0:16].reshape(256, CHANS), preferred_element_type=F32
    )
    for at, (p, q) in enumerate(SIDE_TILES):
        cells[p, q] = spread[at * 16 : (at + 1) * 16].astype(BF16)
    others[sides_at:] = spread[sides_at:]
    convolve_rest(cells, k1, acc, SIDE_TILES)

    for copy in sent[:4]:
        copy.wait_recv()
    norm_halo((
        (16, 1, has_up & has_left), (17, 1, has_up & has_right),
        (18, 1, has_down & has_left), (19, 1, has_down & has_right),
    ))
    spread = others[sides_at:] + jnp.dot(
        g_halo[sides_at:, 256:384], normed[16:24].reshape(128, CHANS), preferred_element_type=F32
    )
    for at, (p, q) in enumerate(CORNER_TILES):
        cells[p, q] = spread[at * 16 : (at + 1) * 16].astype(BF16)
    convolve_rest(cells, k1, acc, CORNER_TILES)

    value = joined(acc, 5, 5)
    value = value / (1.0 + jnp.exp(-value))
    def flag(there):
        return jnp.where(there, 1.0, 0.0).astype(F32)

    j_of = lax.broadcasted_iota(jnp.int32, (1, 8, CHANS), 1) % 2
    sides = jnp.where(j_of == 0, flag(has_left), flag(has_right))
    inner, below = value[0:4], value[4]
    top = jnp.stack([below[:, 0] * flag(has_up), inner[3][:, 0]], axis=1)
    bottom = jnp.stack([inner[0][:, 1], below[:, 1] * flag(has_down)], axis=1)
    for p, line in enumerate((top, inner[0], inner[1], inner[2], inner[3], bottom)):
        edge = line[4] * sides
        first = jnp.where(j_of == 0, edge, pltpu.roll(line[3], 1, 1))
        last = jnp.where(j_of == 1, edge, pltpu.roll(line[0], 7, 1))
        for q, tile in enumerate((first, line[0], line[1], line[2], line[3], last)):
            hidden[p, q] = tile.reshape(16, CHANS).astype(BF16)

    load_k2.wait()

    def mix(half):
        convolve(hidden, k2, acc, half)
        before = kept[128 * half : 128 * half + 128].reshape(2, 4, 2, 8, CHANS)
        mixed = (before + joined(acc, 2, 4)).astype(BF16).reshape(8, 16, CHANS)
        for tile in range(8):
            lat[8 * half + tile, zh, y] = mixed[tile]

    zs = [zh] + [lax.rem(zh + step, RING) for step in (1, 2, 3)]
    ys = [y] + [lax.rem(y + step, RING) for step in (1, 2, 3)]
    pending = []
    near, far, near2, far2 = {}, {}, {}, {}

    def pieces(c, u, v, part=None):
        first, last, y_first = PARTS[c]
        if part is not None:
            middle = (first + last) // 2
            first, last = (first, middle) if part == 0 else (middle, last)
        a, b = (zs[v], ys[u]) if y_first else (zs[u], ys[v])
        return lat.at[pl.ds(first, last - first), a, b]

    def straight(c, u):
        return any(move == "D%d%d" % (c, u) for move in ORDER)

    def pass_on(piece, send_sem, recv_sem, device):
        copy = send(piece, piece, send_sem, recv_sem, device)
        pending.append(copy)
        return copy

    def multiply(c, which, taps):
        first, last, y_first = PARTS[c]
        for b in taps:
            part = None
            for tile in range(first, last):
                block = jnp.concatenate(
                    [(lat[tile, :, ys[u]] if y_first else lat[tile, zs[u]]).reshape(64, CHANS) for u in which], axis=0
                )
                term = lax.dot_general(
                    block,
                    w[b, :, tile * CHANS : (tile + 1) * CHANS],
                    (((1,), (1,)), ((), ())),
                    preferred_element_type=F32,
                )
                part = term if part is None else part + term
            for at, u in enumerate(which):
                term = part[at * 64 : (at + 1) * 64].reshape(RING, 16, 3 * OUT_DEV)
                if y_first:
                    y_acc[b, :, ys[u]] += term
                else:
                    y_acc[b, zs[u]] += term

    for move in ORDER:
        what, c, u = move[0], int(move[1]), int(move[2:3] or 0)
        if what == "C":
            mix(c)
            continue
        rings = (to_y, to_z) if PARTS[c][2] else (to_z, to_y)
        opposite = (to_y2, to_z2) if PARTS[c][2] else (to_z2, to_y2)
        if what == "n":
            near[c] = [
                pass_on(pieces(c, 0, 0), near_send.at[c, d], near_recv.at[c, d], rings[0][d]) for d in range(2)
            ]
        elif what == "f":
            for copy in near[c]:
                copy.wait_recv()
            far[c] = [
                pass_on(pieces(c, 3 - 2 * d, 0, d), far_send.at[c, d], far_recv.at[c, d], rings[0][d]) for d in range(2)
            ]
        elif what == "d":
            far[c] = [pass_on(pieces(c, 0, 0), far_send.at[c, 0], far_recv.at[c, 0], opposite[0])]
        elif what == "e":
            for copy in near[c]:
                copy.wait_recv()
        elif what in "ND":
            if u == 2:
                for copy in far[c]:
                    copy.wait_recv()
            near2[c, u] = [
                pass_on(pieces(c, u, 0), near2_send.at[c, u, d], near2_recv.at[c, u, d], rings[1][d]) for d in range(2)
            ]
            if what == "D":
                far2[c, u] = pass_on(pieces(c, u, 0), far2_send.at[c, u], far2_recv.at[c, u], opposite[1])
        elif what == "F":
            for copy in near2[c, u]:
                copy.wait_recv()
            d = (0, 1, 1, 0)[u] if c % 2 == 0 else (1, 1, 0, 0)[u]
            far2[c, u] = pass_on(pieces(c, u, 3 - 2 * d), far2_send.at[c, u], far2_recv.at[c, u], rings[1][d])
        else:
            for copy in w_loads:
                copy.wait()
            w_loads = []
            which = [int(u) for u in move[2:]]
            for u in which:
                if straight(c, u):
                    for copy in near2[c, u]:
                        copy.wait_recv()
                far2[c, u].wait_recv()
            multiply(c, which, (0, 2))

    s = lax.broadcasted_iota(jnp.int32, (1, 16, OUT_DEV), 1) % 2
    edge = jnp.zeros((1, 16, OUT_DEV), F32)

    def moved(b):
        sums = y_acc[b].reshape(PIECES, 16, 3 * OUT_DEV)
        first, second, third = (sums[..., e * OUT_DEV : (e + 1) * OUT_DEV] for e in range(3))
        from_left = jnp.concatenate([edge, pltpu.roll(first, 15, 1)[: PIECES - 1]], axis=0)
        from_right = jnp.concatenate([pltpu.roll(third, 1, 1)[1:], edge], axis=0)
        total = second + jnp.where(s == 1, pltpu.roll(first, 1, 1), from_left)
        total += jnp.where(s == 0, pltpu.roll(third, 15, 1), from_right)
        return total.reshape(PIECES, 2, 8, OUT_DEV)

    def pack(part):
        return jnp.concatenate([part[:8].reshape(64, OUT_DEV), part[8:].reshape(64, OUT_DEV)], axis=1)

    above, below = moved(0), moved(2)
    u_out[0] = pack(below[:, 0])
    u_out[1] = pack(above[:, 1])
    rows_sent = [
        send(u_out.at[0], u_in.at[1], u_send.at[0], u_recv.at[0], (up, col)),
        send(u_out.at[1], u_in.at[0], u_send.at[1], u_recv.at[1], (down, col)),
    ]
    for c in range(CHUNKS):
        multiply(c, range(RING), (1,))
    load_mean.wait()
    centre = lat[col].reshape(256, CHANS)
    shortcut = jnp.dot(centre, g_mean[...], preferred_element_type=F32).reshape(PIECES, 2, 8, OUT_DEV)
    same = moved(1) + shortcut
    result0 = same[:, 0] + below[:, 1]
    result1 = same[:, 1] + above[:, 0]

    for copy in rows_sent:
        copy.wait_recv()

    def unpack(part, there):
        part = jnp.where(there, part, 0.0)
        return jnp.concatenate(
            [part[:, :OUT_DEV].reshape(8, 8, OUT_DEV), part[:, OUT_DEV:].reshape(8, 8, OUT_DEV)], axis=0
        )

    out_ref[0] = (result0 + unpack(u_in[0], has_up)).reshape(128, OUT_DEV).astype(BF16)
    out_ref[1] = (result1 + unpack(u_in[1], has_down)).reshape(128, OUT_DEV).astype(BF16)
    for copy in sent + pending + rows_sent:
        copy.wait_send()


def per_device(n_row, n_col, frames_in, norm_gain, first_kernel, second_kernel, latent_kernel):
    g_own, g_halo = spread_tables()
    anywhere = pl.BlockSpec(memory_space=pltpu.HBM)
    dma = pltpu.SemaphoreType.DMA
    out = pl.pallas_call(
        functools.partial(kernel, n_row, n_col),
        out_shape=jax.ShapeDtypeStruct((2, 128, OUT_DEV), BF16),
        in_specs=[anywhere] * 9,
        out_specs=pl.BlockSpec(memory_space=pltpu.VMEM),
        scratch_shapes=[
            pltpu.VMEM((4, 4, 16, CHANS), BF16),
            pltpu.VMEM((1, CHANS), F32),
            pltpu.VMEM((3, 3, 3, CHANS, CHANS), BF16),
            pltpu.VMEM((3, 3, 3, CHANS, CHANS), BF16),
            pltpu.VMEM((3, 3 * OUT_DEV, LATENT), BF16),
            pltpu.VMEM((81 * 16, 256), BF16),
            pltpu.VMEM((65 * 16, 384), BF16),
            pltpu.VMEM((128, 256), BF16),
            pltpu.VMEM((CHANS, OUT_DEV), BF16),
            pltpu.VMEM((2, 4, 16, CHANS), BF16),
            pltpu.VMEM((20, 16, CHANS), BF16),
            pltpu.VMEM((24, 16, CHANS), BF16),
            pltpu.VMEM((9, 9, 16, CHANS), BF16),
            pltpu.VMEM((65 * 16, CHANS), F32),
            pltpu.VMEM((6, 6, 16, CHANS), BF16),
            pltpu.VMEM((3, 5, 5, 16, CHANS), F32),
            pltpu.VMEM((PIECES, RING, RING, 16, CHANS), BF16),
            pltpu.VMEM((3, RING, RING, 16, 3 * OUT_DEV), F32),
            pltpu.VMEM((2, 64, 2 * OUT_DEV), F32),
            pltpu.VMEM((2, 64, 2 * OUT_DEV), F32),
            pltpu.VMEM((256, CHANS), F32),
            dma((8,)),
            dma((3,)),
            dma((8,)),
            dma((8,)),
            dma((CHUNKS, 2)),
            dma((CHUNKS, 2)),
            dma((CHUNKS, 2)),
            dma((CHUNKS, 2)),
            dma((CHUNKS, RING, 2)),
            dma((CHUNKS, RING, 2)),
            dma((CHUNKS, RING)),
            dma((CHUNKS, RING)),
            dma((2,)),
            dma((2,)),
        ],
        compiler_params=pltpu.CompilerParams(
            collective_id=0, has_side_effects=True, vmem_limit_bytes=60 << 20
        ),
        cost_estimate=pl.CostEstimate(flops=4 << 30, bytes_accessed=14 << 20, transcendentals=1 << 18),
    )(
        frames_in.reshape(4, 4, 16, CHANS),
        norm_gain.reshape(1, CHANS),
        first_kernel,
        second_kernel,
        latent_kernel.transpose(0, 1, 3, 2).reshape(3, 3 * OUT_DEV, LATENT),
        g_own,
        g_halo,
        strip_table(),
        mean_table(),
    )
    out = out.reshape(2, PIECES, FRAMES, 2, OUT_DEV)
    return out.transpose(2, 0, 1, 3, 4).reshape(FRAMES, 2, 2 * PIECES, OUT_DEV)


def solution(mesh):
    return jax.shard_map(
        functools.partial(per_device, mesh.shape["row"], mesh.shape["col"]),
        mesh=mesh,
        in_specs=(P(None, "row", "col", None), P(), P(), P(), P(None, None, None, "col")),
        out_specs=P(None, "row", None, "col"),
        check_vma=False,
    )
```
